256 devices in a mesh: seq: 32 (over z, y), ch: 8 (over x, core).
Axes of the slice: x: 4, y: 4, z: 8, core: 2. Of those that a mesh axis runs over, the one named last changes fastest.
Arguments:
- tokens: bfloat16 [8192, 4096], P('seq'), may hold values from -6 to 6
- in_weight: bfloat16 [4096, 3, 2048], P(None, None, 'ch'), may hold values from -0.09375 to 0.09375
- filter_taps: float32 [8192, 2048], P('seq', 'ch'), may hold values from -120 to 120
- skip_gain: float32 [2048], P('ch'), may hold values from -1 to 1
- out_weight: bfloat16 [2048, 4096], P(None, 'ch'), may hold values from -0.125 to 0.125
- grad_out: bfloat16 [8192, 4096], P('seq', 'ch'), may hold values from -6 to 6
Outputs:
- output: bfloat16 [8192, 4096], P('seq', 'ch')
- grad_tokens: bfloat16 [8192, 4096], P('seq', 'ch')
- grad_taps: float32 [8192, 2048], P('seq', 'ch')
The draws below stay inside these ranges and needn't reach their ends.
All inputs are finite; a program needn't handle non-finite values.
Results may differ from the reference program's by a relative error of at most 0.019.
Values may be sent and summed in bfloat16 or wider, within the bound.
A program may use at most 128 MiB of HBM per device.

```python
import math
import jax
import jax.numpy as jnp

D = 4096
CH = 2048
LENGTH = 8192


def draw_filter_taps(key, part):
    key = jax.random.fold_in(key, 1)
    rate_key, noise_key = jax.random.split(key)
    position = jnp.arange(LENGTH, dtype=jnp.float32)[:, None] / LENGTH
    rate = jnp.exp(jax.random.uniform(rate_key, (CH,), jnp.float32, math.log(0.3), math.log(200.0)))
    noise = jnp.clip(jax.random.normal(noise_key, (LENGTH, CH), jnp.float32), -6.0, 6.0)
    return noise * jnp.exp(-rate[None, :] * position) * jnp.sqrt(2.0 * rate)[None, :]


def levels(key, dims, shards, least, top_value):
    def one(dim, shards_of):
        draws = jax.random.uniform(jax.random.fold_in(jax.random.fold_in(key, 6), dim), (shards_of,), jnp.float32, least / len(shards), top_value / len(shards))
        return jnp.repeat(jnp.exp(draws), dims[dim] // shards_of).reshape((-1,) + (1,) * (len(dims) - dim - 1))

    factor_of = one(*shards[0])
    for cut in shards[1:]:
        factor_of = factor_of * one(*cut)
    return factor_of


def normal_values(own_key, shape, deviation, bound, cuts=(), kind=jnp.bfloat16):
    values = deviation * jax.random.normal(own_key, shape, jnp.float32)
    if cuts:
        values = values * levels(own_key, shape, cuts, -0.22, 0.18)
    return jnp.clip(values, -bound, bound).astype(kind)


def setup_inputs(seed: int = 0) -> dict:
    splits = jax.random.split(jax.random.key(seed), 7)
    return {
        "tokens": normal_values(splits[0], (LENGTH, D), 1.0, 6.0, ((0, 32),)),
        "in_weight": normal_values(splits[1], (D, 3, CH), D ** -0.5, 0.09375, ((2, 8),)),
        "filter_taps": draw_filter_taps(jax.random.fold_in(splits[6], 71), 0),
        "skip_gain": jnp.clip(jax.random.uniform(splits[3], (CH,), jnp.float32, -1.0, 1.0) * levels(splits[3], (CH,), ((0, 8),), -0.4, 0.0), -1.0, 1.0),
        "out_weight": normal_values(splits[4], (CH, D), CH ** -0.5, 0.125, ((1, 8),)),
        "grad_out": normal_values(splits[5], (LENGTH, D), 1.0, 6.0, ((0, 32), (1, 8))),
    }


def reference(tokens, in_weight, filter_taps, skip_gain, out_weight, grad_out):
    length = tokens.shape[0]
    padded = 2 * length
    width = tokens.shape[1]
    channels = in_weight.shape[2]
    flat_in = in_weight.reshape(width, 3 * channels)
    mixed = jnp.dot(tokens, flat_in, preferred_element_type=jnp.float32).astype(jnp.bfloat16)
    mixed = mixed.reshape(length, 3, channels).astype(jnp.float32)
    value = mixed[:, 0, :]
    gate_one = mixed[:, 1, :]
    gate_two = mixed[:, 2, :]
    scale = jnp.float32(length) ** -0.5
    taps = filter_taps * scale
    pre = gate_one * value
    spec_taps = jnp.fft.rfft(taps, n=padded, axis=0)
    spec_pre = jnp.fft.rfft(pre, n=padded, axis=0)
    conv = jnp.fft.irfft(spec_taps * spec_pre, n=padded, axis=0)[:length] + skip_gain * pre
    gated = (gate_two * conv).astype(jnp.bfloat16)
    output = jnp.dot(gated, out_weight, preferred_element_type=jnp.float32).astype(jnp.bfloat16)
    grad_gated = jnp.dot(grad_out, out_weight.T, preferred_element_type=jnp.float32)
    grad_conv = grad_gated * gate_two
    grad_gate_two = grad_gated * conv
    spec_grad = jnp.fft.rfft(grad_conv, n=padded, axis=0)
    grad_pre = jnp.fft.irfft(jnp.conj(spec_taps) * spec_grad, n=padded, axis=0)[:length] + skip_gain * grad_conv
    grad_taps = jnp.fft.irfft(jnp.conj(spec_pre) * spec_grad, n=padded, axis=0)[:length] * scale
    grad_mixed = jnp.stack([grad_pre * gate_one, grad_pre * value, grad_gate_two], axis=1)
    grad_mixed = grad_mixed.astype(jnp.bfloat16).reshape(length, 3 * channels)
    grad_tokens = jnp.dot(grad_mixed, flat_in.T, preferred_element_type=jnp.float32).astype(jnp.bfloat16)
    return output, grad_tokens, grad_taps
```

```python
import functools
import math

import jax
import jax.numpy as jnp
import ml_dtypes
import numpy as np
from jax import lax
from jax.experimental import pallas as pl
from jax.experimental.pallas import tpu as pltpu
from jax.sharding import PartitionSpec as P

MESH = pl.DeviceIdType.MESH
F32 = jnp.float32
BF16 = jnp.bfloat16
LANES = 128


def tables(ranks, per):
    rows = 2 * ranks
    length = rows * LANES
    first = np.arange(rows)
    low = first + 0.25
    angle = 2.0 * np.pi * np.outer(low, first) / rows
    eye = np.eye(per)
    cross = np.concatenate(
        [np.kron(np.cos(angle), eye), np.kron(-np.sin(angle), eye)], axis=0
    )
    cross_back = cross.T / length
    turn = 2.0 * np.pi * np.outer(np.repeat(low, per), np.arange(LANES)) / length
    inner = 2.0 * np.pi * np.outer(np.arange(LANES), np.arange(LANES)) / LANES
    cosine, sine = np.cos(inner), np.sin(inner)
    local = np.block([[cosine, -sine], [sine, cosine]])
    narrow = ml_dtypes.bfloat16
    return (
        cross.astype(narrow),
        cross_back.astype(narrow),
        local.astype(narrow),
        local.T.astype(narrow),
        np.cos(turn).astype(np.float32),
        (-np.sin(turn)).astype(np.float32),
    )


def dot(left, right):
    return jnp.dot(left, right, preferred_element_type=F32)


def dot_nt(left, right):
    return lax.dot_general(
        left, right, (((1,), (1,)), ((), ())), preferred_element_type=F32
    )


def kernel(
    ranks,
    chans,
    *refs,
):
    (
        tok_h, win_h, taps_h, skip_ref, wout_h, gout_h,
        cross_h, back_h, local_h, unlocal_h, tr_h, ti_h,
        out_h, gtok_h, gtaps_h,
        tok, win, taps, wout, gout, cross, back, local, unlocal, tr, ti,
        mixed, pre, gg, gc, spec_t, spec_p,
        s_taps, s_pre, s_grad, s_conv, s_gpre, s_gtaps,
        r_taps, r_pre, r_grad, r_conv, r_gpre, r_gtaps,
        a_send, a_got, a_own, a_sum, a_part,
        gath, gm,
        b_send, b_got, b_own, b_sum, b_part,
        o_out, o_gtok, o_gtaps,
        load_sem, store_sem, seq_send, seq_recv,
        pair_send, a_sem, b_sem, x_send, a_x_sem, b_x_sem,
        ag_send, ag_sem,
    ) = refs
    seq = lax.axis_index("seq")
    ch = lax.axis_index("ch")
    chips = chans // 2
    x, core = ch // 2, ch % 2
    partner = (seq, ch + 1 - 2 * core)
    block, width = tok.shape
    local_ch = win.shape[2]
    per = local_ch // ranks
    feats = gout.shape[1]
    half = ranks * 2 * per
    scale = (ranks * block) ** -0.5

    def peer(step):
        return (x + step) % chips

    order = [k for k in (2, 1, 3) if k < chips]

    loads = [
        (gout_h, gout), (wout_h, wout), (taps_h, taps), (tok_h, tok),
        (win_h.at[0], win.at[0]), (win_h.at[1], win.at[1]), (win_h.at[2], win.at[2]),
        (cross_h, cross), (local_h, local), (tr_h, tr), (ti_h, ti),
        (unlocal_h, unlocal), (back_h, back),
    ]
    copies = [
        pltpu.make_async_copy(src, dst, load_sem.at[i])
        for i, (src, dst) in enumerate(loads)
    ]
    for copy in copies:
        copy.start()

    barrier = pltpu.get_barrier_semaphore()

    def greet(k, carry):
        pl.semaphore_signal(
            barrier, inc=1, device_id=((seq + k) % ranks, ch), device_id_type=MESH
        )
        return carry

    lax.fori_loop(1, ranks, greet, 0)
    pl.semaphore_signal(barrier, inc=1, device_id=partner, device_id_type=MESH)
    for k in order:
        pl.semaphore_signal(
            barrier, inc=1, device_id=(seq, 2 * peer(k) + core), device_id_type=MESH
        )

    def remote(src, dst, send, recv, device):
        copy = pltpu.make_async_remote_copy(
            src_ref=src, dst_ref=dst, send_sem=send, recv_sem=recv,
            device_id=device, device_id_type=MESH,
        )
        copy.start()

    def wait(ref, sem):
        pltpu.make_async_copy(ref, ref, sem).wait()

    def spread(buf, got, n):
        def send(k, carry):
            to = (seq + k) % ranks
            remote(buf.at[to], got.at[seq], seq_send.at[n], seq_recv.at[n], (to, ch))
            return carry

        lax.fori_loop(1, ranks, send, 0)
        got[seq] = buf[seq]

    def arrive(got, n):
        wait(got.at[pl.ds(0, ranks - 1)], seq_recv.at[n])

    def to_pieces(value, buf):
        turned = value.T
        parts = [
            turned[:, i * LANES : (i + 1) * LANES].reshape(ranks, per, LANES)
            for i in range(2)
        ]
        buf[...] = jnp.concatenate(parts, axis=1).astype(BF16)

    def from_pieces(got):
        parts = got[...].astype(F32)
        turned = jnp.concatenate(
            [
                parts[:, i * per : (i + 1) * per, :].reshape(local_ch, LANES)
                for i in range(2)
            ],
            axis=1,
        )
        return turned.T

    def spectrum(got):
        flat = got[...].reshape(half, LANES)
        both = dot(cross[...], flat)
        re, im = both[:half], both[half:]
        cosine, sine = tr[...], ti[...]
        turned = jnp.concatenate(
            [re * cosine - im * sine, re * sine + im * cosine], axis=1
        )
        return dot(turned.astype(BF16), local[...])

    def inverse(re, im, buf):
        both = dot(jnp.concatenate([re, im], axis=1).astype(BF16), unlocal[...])
        re, im = both[:, :LANES], both[:, LANES:]
        cosine, sine = tr[...], ti[...]
        turned = jnp.concatenate(
            [re * cosine + im * sine, im * cosine - re * sine], axis=0
        )
        result = dot(back[...], turned.astype(BF16))
        buf[...] = result.astype(BF16).reshape(ranks, 2 * per, LANES)

    copies[0].wait()
    copies[1].wait()

    def feature_chunk(index):
        rows = wout[pl.ds(pl.multiple_of(index * local_ch, local_ch), local_ch), :]
        return dot_nt(gout[...], rows)

    for i, k in enumerate(order + [0]):
        to = peer(k)
        a_send[to] = feature_chunk(2 * to + 1 - core).astype(BF16)
        if i == 0:
            pl.semaphore_wait(barrier, ranks - 1 + 1 + len(order))
        remote(a_send.at[to], a_got.at[to], pair_send.at[0], a_sem.at[to], partner)
    for k in order + [0]:
        to = peer(k)
        a_own[to] = feature_chunk(2 * to + core)

    copies[2].wait()
    to_pieces(taps[...] * scale, s_taps)

    for k in order:
        to = peer(k)
        wait(a_got.at[to], a_sem.at[to])
        a_sum[to] = (a_own[to] + a_got[to].astype(F32)).astype(BF16)
        remote(
            a_sum.at[to], a_part.at[x], x_send.at[0], a_x_sem.at[x], (seq, 2 * to + core)
        )

    spread(s_taps, r_taps, 0)

    for i in (3, 4, 5, 6):
        copies[i].wait()

    def project(i, carry):
        mixed[i] = dot(tok[...], win[i]).astype(BF16)
        return carry

    lax.fori_loop(0, 3, project, 0)
    pre[...] = mixed[1].astype(F32) * mixed[0].astype(F32)
    to_pieces(pre[...], s_pre)
    spread(s_pre, r_pre, 1)

    wait(a_got.at[x], a_sem.at[x])
    gg[...] = a_own[x] + a_got[x].astype(F32)
    for k in (1, 3, 2):
        if k < chips:
            wait(a_part.at[peer(k)], a_x_sem.at[peer(k)])
            gg[...] += a_part[peer(k)].astype(F32)
    gc[...] = gg[...] * mixed[2].astype(F32)
    to_pieces(gc[...], s_grad)
    spread(s_grad, r_grad, 2)

    for i in range(7, 13):
        copies[i].wait()
    arrive(r_taps, 0)
    spec_t[...] = spectrum(r_taps)
    arrive(r_pre, 1)
    spec_p[...] = spectrum(r_pre)
    t_re, t_im = spec_t[:, :LANES], spec_t[:, LANES:]
    p_re, p_im = spec_p[:, :LANES], spec_p[:, LANES:]
    inverse(t_re * p_re - t_im * p_im, t_re * p_im + t_im * p_re, s_conv)
    spread(s_conv, r_conv, 3)
    arrive(r_grad, 2)
    spec_g = spectrum(r_grad)
    g_re, g_im = spec_g[:, :LANES], spec_g[:, LANES:]
    t_re, t_im = spec_t[:, :LANES], spec_t[:, LANES:]
    inverse(t_re * g_re + t_im * g_im, t_re * g_im - t_im * g_re, s_gpre)
    spread(s_gpre, r_gpre, 4)
    p_re, p_im = spec_p[:, :LANES], spec_p[:, LANES:]
    inverse(p_re * g_re + p_im * g_im, p_re * g_im - p_im * g_re, s_gtaps)
    spread(s_gtaps, r_gtaps, 5)

    arrive(r_conv, 3)
    conv = from_pieces(r_conv) + skip_ref[...] * pre[...]
    gath[ch] = (mixed[2].astype(F32) * conv).astype(BF16)
    for k in order:
        remote(
            gath.at[ch], gath.at[ch], ag_send, ag_sem.at[ch], (seq, 2 * peer(k) + core)
        )
    remote(gath.at[ch], gath.at[ch], ag_send, ag_sem.at[ch], partner)
    gm[2] = (gg[...] * conv).astype(BF16)

    arrive(r_gpre, 4)
    grad_pre = from_pieces(r_gpre) + skip_ref[...] * gc[...]
    gm[0] = (grad_pre * mixed[1].astype(F32)).astype(BF16)
    gm[1] = (grad_pre * mixed[0].astype(F32)).astype(BF16)

    def input_chunk(index):
        rows = pl.ds(pl.multiple_of(index * feats, feats), feats)
        total = dot_nt(gm[0], win[0, rows, :])
        total += dot_nt(gm[1], win[1, rows, :])
        return total + dot_nt(gm[2], win[2, rows, :])

    for k in order + [0]:
        to = peer(k)
        b_send[to] = input_chunk(2 * to + 1 - core).astype(BF16)
        remote(b_send.at[to], b_got.at[to], pair_send.at[1], b_sem.at[to], partner)
    for k in order:
        to = peer(k)
        b_own[to] = input_chunk(2 * to + core)
        wait(b_got.at[to], b_sem.at[to])
        b_sum[to] = (b_own[to] + b_got[to].astype(F32)).astype(BF16)
        remote(
            b_sum.at[to], b_part.at[x], x_send.at[1], b_x_sem.at[x], (seq, 2 * to + core)
        )
    for k in (1, 3, 2):
        if k < chips:
            slot = 2 * peer(k) + core
            wait(gath.at[slot], ag_sem.at[slot])
            remote(gath.at[slot], gath.at[slot], ag_send, ag_sem.at[slot], partner)
    b_own[x] = input_chunk(2 * x + core)

    for k in range(chips):
        slot = 2 * peer(k) + 1 - core
        wait(gath.at[slot], ag_sem.at[slot])

    def output_rows(index):
        rows = wout[pl.ds(pl.multiple_of(index * local_ch, local_ch), local_ch), :]
        return dot(gath[index], rows)

    total = output_rows(0)
    for i in range(1, chans):
        total += output_rows(i)
    o_out[...] = total.astype(BF16)
    out_copy = pltpu.make_async_copy(o_out, out_h, store_sem.at[0])
    out_copy.start()

    arrive(r_gtaps, 5)
    o_gtaps[...] = from_pieces(r_gtaps) * scale
    gtaps_copy = pltpu.make_async_copy(o_gtaps, gtaps_h, store_sem.at[1])
    gtaps_copy.start()

    wait(b_got.at[x], b_sem.at[x])
    b_own[x] += b_got[x].astype(F32)
    for k in (1, 3, 2):
        if k < chips:
            wait(b_part.at[peer(k)], b_x_sem.at[peer(k)])
            b_own[x] += b_part[peer(k)].astype(F32)
    o_gtok[...] = b_own[x].astype(BF16)
    gtok_copy = pltpu.make_async_copy(o_gtok, gtok_h, store_sem.at[2])
    gtok_copy.start()

    for n, buf in enumerate((s_taps, s_pre, s_grad, s_conv, s_gpre, s_gtaps)):
        wait(buf.at[pl.ds(0, ranks - 1)], seq_send.at[n])
    wait(a_send, pair_send.at[0])
    wait(b_send, pair_send.at[1])
    if order:
        wait(a_sum.at[pl.ds(0, len(order))], x_send.at[0])
        wait(b_sum.at[pl.ds(0, len(order))], x_send.at[1])
    wait(gath.at[pl.ds(0, 2 * len(order) + 1)], ag_send)
    out_copy.wait()
    gtaps_copy.wait()
    gtok_copy.wait()


def on_device(ranks, chans, tokens, in_weight, filter_taps, skip_gain, out_weight, grad_out):
    block, width = tokens.shape
    local_ch = in_weight.shape[2]
    feats = grad_out.shape[1]
    per = local_ch // ranks
    chips = chans // 2
    half = 2 * ranks * per
    weight = jnp.transpose(in_weight, (1, 0, 2))
    constants = tables(ranks, per)
    hbm = pl.BlockSpec(memory_space=pl.ANY)
    vmem = pl.BlockSpec(memory_space=pltpu.VMEM)
    piece = (ranks, 2 * per, LANES)
    chunk = (chips, block, local_ch)
    wide = (chips, block, feats)
    scratch = [
        pltpu.VMEM(tokens.shape, BF16),
        pltpu.VMEM(weight.shape, BF16),
        pltpu.VMEM(filter_taps.shape, F32),
        pltpu.VMEM(out_weight.shape, BF16),
        pltpu.VMEM(grad_out.shape, BF16),
        pltpu.VMEM((2 * half, half), BF16),
        pltpu.VMEM((half, 2 * half), BF16),
        pltpu.VMEM((2 * LANES, 2 * LANES), BF16),
        pltpu.VMEM((2 * LANES, 2 * LANES), BF16),
        pltpu.VMEM((half, LANES), F32),
        pltpu.VMEM((half, LANES), F32),
        pltpu.VMEM((3, block, local_ch), BF16),
        pltpu.VMEM((block, local_ch), F32),
        pltpu.VMEM((block, local_ch), F32),
        pltpu.VMEM((block, local_ch), F32),
        pltpu.VMEM((half, 2 * LANES), F32),
        pltpu.VMEM((half, 2 * LANES), F32),
        *[pltpu.VMEM(piece, BF16) for _ in range(12)],
        pltpu.VMEM(chunk, BF16),
        pltpu.VMEM(chunk, BF16),
        pltpu.VMEM(chunk, F32),
        pltpu.VMEM(chunk, BF16),
        pltpu.VMEM(chunk, BF16),
        pltpu.VMEM((chans, block, local_ch), BF16),
        pltpu.VMEM((3, block, local_ch), BF16),
        pltpu.VMEM(wide, BF16),
        pltpu.VMEM(wide, BF16),
        pltpu.VMEM(wide, F32),
        pltpu.VMEM(wide, BF16),
        pltpu.VMEM(wide, BF16),
        pltpu.VMEM((block, feats), BF16),
        pltpu.VMEM((block, feats), BF16),
        pltpu.VMEM((block, local_ch), F32),
        pltpu.SemaphoreType.DMA((13,)),
        pltpu.SemaphoreType.DMA((3,)),
        pltpu.SemaphoreType.DMA((6,)),
        pltpu.SemaphoreType.DMA((6,)),
        pltpu.SemaphoreType.DMA((2,)),
        pltpu.SemaphoreType.DMA((chips,)),
        pltpu.SemaphoreType.DMA((chips,)),
        pltpu.SemaphoreType.DMA((2,)),
        pltpu.SemaphoreType.DMA((chips,)),
        pltpu.SemaphoreType.DMA((chips,)),
        pltpu.SemaphoreType.DMA,
        pltpu.SemaphoreType.DMA((chans,)),
    ]
    return pl.pallas_call(
        functools.partial(kernel, ranks, chans),
        out_shape=(
            jax.ShapeDtypeStruct((block, feats), BF16),
            jax.ShapeDtypeStruct((block, feats), BF16),
            jax.ShapeDtypeStruct((block, local_ch), F32),
        ),
        in_specs=[hbm, hbm, hbm, vmem, hbm, hbm] + [hbm] * 6,
        out_specs=(hbm, hbm, hbm),
        scratch_shapes=scratch,
        compiler_params=pltpu.CompilerParams(
            collective_id=0, has_side_effects=True, vmem_limit_bytes=58 * 1024 * 1024
        ),
    )(
        tokens, weight, filter_taps, skip_gain.reshape(1, local_ch), out_weight, grad_out,
        *[jnp.asarray(table) for table in constants],
    )


def solution(mesh):
    placed = (
        P("seq", None),
        P(None, None, "ch"),
        P("seq", "ch"),
        P("ch"),
        P(None, "ch"),
        P("seq", "ch"),
    )
    return jax.shard_map(
        functools.partial(on_device, mesh.shape["seq"], mesh.shape["ch"]),
        mesh=mesh,
        in_specs=placed,
        out_specs=(P("seq", "ch"), P("seq", "ch"), P("seq", "ch")),
        check_vma=False,
    )
```

```python
import functools
import math

import jax
import jax.numpy as jnp
import ml_dtypes
import numpy as np
from jax import lax
from jax.experimental import pallas as pl
from jax.experimental.pallas import tpu as pltpu
from jax.sharding import PartitionSpec as P

MESH = pl.DeviceIdType.MESH
F32 = jnp.float32
BF16 = jnp.bfloat16
LANES = 128


def tables(ranks, per):
    rows = 2 * ranks
    length = rows * LANES
    first = np.arange(rows)
    low = first + 0.25
    angle = 2.0 * np.pi * np.outer(low, first) / rows
    eye = np.eye(per)
    cross = np.concatenate(
        [np.kron(np.cos(angle), eye), np.kron(-np.sin(angle), eye)], axis=0
    )
    cross_back = cross.T / length
    turn = 2.0 * np.pi * np.outer(np.repeat(low, per), np.arange(LANES)) / length
    inner = 2.0 * np.pi * np.outer(np.arange(LANES), np.arange(LANES)) / LANES
    cosine, sine = np.cos(inner), np.sin(inner)
    local = np.block([[cosine, -sine], [sine, cosine]])
    narrow = ml_dtypes.bfloat16
    return (
        cross.astype(narrow),
        cross_back.astype(narrow),
        local.astype(narrow),
        local.T.astype(narrow),
        np.cos(turn).astype(np.float32),
        (-np.sin(turn)).astype(np.float32),
    )


def dot(left, right):
    return jnp.dot(left, right, preferred_element_type=F32)


def dot_nt(left, right):
    return lax.dot_general(
        left, right, (((1,), (1,)), ((), ())), preferred_element_type=F32
    )


def kernel(
    ranks,
    chans,
    *refs,
):
    (
        tok_h, win_h, taps_h, skip_ref, wout_h, gout_h,
        cross_h, back_h, local_h, unlocal_h, tr_h, ti_h,
        out_h, gtok_h, gtaps_h,
        tok, win, taps, wout, gout, cross, back, local, unlocal, tr, ti,
        mixed, pre, gg, gc, spec_t, spec_p, spec_g,
        s_taps, s_pre, s_grad, s_conv, s_gpre, s_gtaps,
        r_taps, r_pre, r_grad, r_conv, r_gpre, r_gtaps,
        a_send, a_got, a_own, a_sum, a_fwd, a_in,
        gath, gm,
        b_send, b_got, b_own, b_sum, b_fwd, b_in,
        o_out, o_gtok, o_gtaps,
        load_sem, store_sem, seq_send, seq_recv,
        pair_send, a_sem, b_sem, x_send, a_f_sem, b_f_sem, a_i_sem, b_i_sem,
        ag_send, ag_sem,
    ) = refs
    seq = lax.axis_index("seq")
    ch = lax.axis_index("ch")
    chips = chans // 2
    x, core = ch // 2, ch % 2
    partner = (seq, ch + 1 - 2 * core)
    block, width = tok.shape
    local_ch = win.shape[2]
    per = local_ch // ranks
    feats = gout.shape[1]
    half = ranks * 2 * per
    scale = (ranks * block) ** -0.5
    part = block // 2
    turns = 4 if ranks % 8 == 0 else 1
    some = ranks // 2

    def peer(step):
        return (x + step) % chips

    def slot_of(rank):
        z, y = rank // turns, rank % turns
        return (z % 2) * some + (z // 2) * turns + y

    def rank_of(slot):
        side, rest = slot // some, slot % some
        return (2 * (rest // turns) + side) * turns + rest % turns

    mine = slot_of(seq)

    loads = [
        (taps_h, taps), (gout_h, gout), (wout_h, wout), (tok_h, tok),
        (win_h.at[0], win.at[0]), (win_h.at[1], win.at[1]), (win_h.at[2], win.at[2]),
        (cross_h, cross), (local_h, local), (tr_h, tr), (ti_h, ti),
        (unlocal_h, unlocal), (back_h, back),
    ]
    copies = [
        pltpu.make_async_copy(src, dst, load_sem.at[i])
        for i, (src, dst) in enumerate(loads)
    ]
    for copy in copies[:3]:
        copy.start()

    barrier = pltpu.get_barrier_semaphore()

    def greet(k, carry):
        pl.semaphore_signal(
            barrier, inc=1, device_id=((seq + k) % ranks, ch), device_id_type=MESH
        )
        return carry

    lax.fori_loop(1, ranks, greet, 0)
    pl.semaphore_signal(barrier, inc=1, device_id=partner, device_id_type=MESH)
    for k in (1, 2, 3):
        pl.semaphore_signal(
            barrier, inc=1, device_id=(seq, 2 * peer(k) + core), device_id_type=MESH
        )

    def remote(src, dst, send, recv, device):
        copy = pltpu.make_async_remote_copy(
            src_ref=src, dst_ref=dst, send_sem=send, recv_sem=recv,
            device_id=device, device_id_type=MESH,
        )
        copy.start()

    def wait(ref, sem):
        pltpu.make_async_copy(ref, ref, sem).wait()

    def spread(buf, got, n):
        def send(k, carry):
            to = (seq + k) % ranks
            remote(
                buf.at[slot_of(to)], got.at[seq], seq_send.at[n], seq_recv.at[n], (to, ch)
            )
            return carry

        lax.fori_loop(1, ranks, send, 0)
        got[seq] = buf[mine]

    def spread_side(buf, got, n, side):
        def send(k, carry):
            slot = side * some + (mine + k) % some
            to = rank_of(slot)

            @pl.when(to != seq)
            def _():
                remote(
                    buf.at[slot], got.at[seq], seq_send.at[n], seq_recv.at[n], (to, ch)
                )

            return carry

        lax.fori_loop(0, some, send, 0)

    def give_back(buf, got, n):
        def send(k, carry):
            to = (seq + k) % ranks
            remote(buf.at[to], got.at[mine], seq_send.at[n], seq_recv.at[n], (to, ch))
            return carry

        lax.fori_loop(1, ranks, send, 0)
        got[mine] = buf[seq]

    def arrive(got, n):
        wait(got.at[pl.ds(0, ranks - 1)], seq_recv.at[n])

    def to_pieces(value, buf, first):
        turned = value.T
        count = turned.shape[0] // per
        parts = [
            turned[:, i * LANES : (i + 1) * LANES].reshape(count, per, LANES)
            for i in range(2)
        ]
        buf[first : first + count] = jnp.concatenate(parts, axis=1).astype(BF16)

    def from_pieces(got):
        parts = got[...].astype(F32)
        turned = jnp.concatenate(
            [
                parts[:, i * per : (i + 1) * per, :].reshape(local_ch, LANES)
                for i in range(2)
            ],
            axis=1,
        )
        return turned.T

    def spectrum(got):
        flat = got[...].reshape(half, LANES)
        both = dot(cross[...], flat)
        re, im = both[:half], both[half:]
        cosine, sine = tr[...], ti[...]
        turned = jnp.concatenate(
            [re * cosine - im * sine, re * sine + im * cosine], axis=1
        )
        return dot(turned.astype(BF16), local[...])

    def inverse(re, im, buf):
        both = dot(jnp.concatenate([re, im], axis=1).astype(BF16), unlocal[...])
        re, im = both[:, :LANES], both[:, LANES:]
        cosine, sine = tr[...], ti[...]
        turned = jnp.concatenate(
            [re * cosine + im * sine, im * cosine - re * sine], axis=0
        )
        result = dot(back[...], turned.astype(BF16))
        buf[...] = result.astype(BF16).reshape(ranks, 2 * per, LANES)

    near = (1, 3)

    def rows(d):
        return pl.ds(d * part, part)

    def columns(ref, h):
        count = ref.shape[-1] // 2
        return slice(h * count, (h + 1) * count)

    def fold(own, got, sem, k):
        to = peer(k)
        wait(got.at[to], sem.at[to])
        own[to] = own[to] + got[to].astype(F32)

    def far(own, sums, fwd, f_sem, n, h):
        sums[0, h] = own[peer(2), :, columns(own, h)].astype(BF16)
        for d in (0, 1):
            remote(
                sums.at[0, h, rows(d)], fwd.at[d, h], x_send.at[n], f_sem.at[d, h],
                (seq, 2 * peer(near[d]) + core),
            )

    def plain(own, sums, into, i_sem, n, h):
        for d in (0, 1):
            to = peer(near[d])
            sums[1 + d, h, rows(1 - d)] = own[
                to, rows(1 - d), columns(own, h)
            ].astype(BF16)
            remote(
                sums.at[1 + d, h, rows(1 - d)], into.at[d, h, rows(1 - d)],
                x_send.at[n], i_sem.at[0, d, h], (seq, 2 * to + core),
            )

    def onward(own, sums, fwd, f_sem, into, i_sem, n, h):
        for d in (0, 1):
            to = peer(near[d])
            wait(fwd.at[d, h], f_sem.at[d, h])
            sums[1 + d, h, rows(d)] = (
                own[to, rows(d), columns(own, h)] + fwd[d, h].astype(F32)
            ).astype(BF16)
            remote(
                sums.at[1 + d, h, rows(d)], into.at[d, h, rows(d)],
                x_send.at[n], i_sem.at[1, d, h], (seq, 2 * to + core),
            )

    def collect(own, into, i_sem, h):
        for d in (0, 1):
            wait(into.at[d, h, rows(1 - d)], i_sem.at[0, d, h])
            wait(into.at[d, h, rows(d)], i_sem.at[1, d, h])
        return own[x, :, columns(own, h)] + (
            into[0, h].astype(F32) + into[1, h].astype(F32)
        )

    copies[0].wait()
    to_pieces(taps[...] * scale, s_taps, 0)
    pl.semaphore_wait(barrier, ranks - 1 + 1 + 3)
    spread(s_taps, r_taps, 0)

    copies[1].wait()
    copies[2].wait()
    for copy in copies[3:7]:
        copy.start()

    def feature_chunk(index):
        weights = wout[pl.ds(pl.multiple_of(index * local_ch, local_ch), local_ch), :]
        return dot_nt(gout[...], weights)

    for k in (2, 1, 3, 0):
        to = peer(k)
        a_send[to] = feature_chunk(2 * to + 1 - core).astype(BF16)
        remote(a_send.at[to], a_got.at[to], pair_send.at[0], a_sem.at[to], partner)
    for k in (2, 1, 3, 0):
        to = peer(k)
        a_own[to] = feature_chunk(2 * to + core)
    fold(a_own, a_got, a_sem, 2)
    far(a_own, a_sum, a_fwd, a_f_sem, 0, 0)
    fold(a_own, a_got, a_sem, 1)
    fold(a_own, a_got, a_sem, 3)
    plain(a_own, a_sum, a_in, a_i_sem, 0, 0)
    far(a_own, a_sum, a_fwd, a_f_sem, 0, 1)
    fold(a_own, a_got, a_sem, 0)

    copies[3].wait()
    copies[4].wait()
    mixed[0] = dot(tok[...], win[0]).astype(BF16)
    onward(a_own, a_sum, a_fwd, a_f_sem, a_in, a_i_sem, 0, 0)
    plain(a_own, a_sum, a_in, a_i_sem, 0, 1)
    copies[5].wait()
    copies[6].wait()
    for copy in copies[7:]:
        copy.start()
    mixed[1] = dot(tok[...], win[1]).astype(BF16)
    onward(a_own, a_sum, a_fwd, a_f_sem, a_in, a_i_sem, 0, 1)
    pre[...] = mixed[1].astype(F32) * mixed[0].astype(F32)
    to_pieces(pre[...], s_pre, 0)
    spread(s_pre, r_pre, 1)
    mixed[2] = dot(tok[...], win[2]).astype(BF16)

    for h in (0, 1):
        cut = columns(gg, h)
        gg[:, cut] = collect(a_own, a_in, a_i_sem, h)
        gc[:, cut] = gg[:, cut] * mixed[2, :, cut].astype(F32)
        to_pieces(gc[:, cut], s_grad, h * some)
        spread_side(s_grad, r_grad, 2, h)
    r_grad[seq] = s_grad[mine]

    for copy in copies[7:]:
        copy.wait()
    arrive(r_taps, 0)
    spec_t[...] = spectrum(r_taps)
    arrive(r_pre, 1)
    spec_p[...] = spectrum(r_pre)
    t_re, t_im = spec_t[:, :LANES], spec_t[:, LANES:]
    p_re, p_im = spec_p[:, :LANES], spec_p[:, LANES:]
    inverse(t_re * p_re - t_im * p_im, t_re * p_im + t_im * p_re, s_conv)
    give_back(s_conv, r_conv, 3)
    arrive(r_grad, 2)
    spec_g[...] = spectrum(r_grad)
    g_re, g_im = spec_g[:, :LANES], spec_g[:, LANES:]
    t_re, t_im = spec_t[:, :LANES], spec_t[:, LANES:]
    inverse(t_re * g_re + t_im * g_im, t_re * g_im - t_im * g_re, s_gpre)
    give_back(s_gpre, r_gpre, 4)
    p_re, p_im = spec_p[:, :LANES], spec_p[:, LANES:]
    g_re, g_im = spec_g[:, :LANES], spec_g[:, LANES:]
    inverse(p_re * g_re + p_im * g_im, p_re * g_im - p_im * g_re, s_gtaps)

    arrive(r_conv, 3)
    conv = from_pieces(r_conv) + skip_ref[...] * pre[...]
    gath[ch] = (mixed[2].astype(F32) * conv).astype(BF16)
    for k in (2, 1, 3):
        remote(
            gath.at[ch], gath.at[ch], ag_send, ag_sem.at[ch], (seq, 2 * peer(k) + core)
        )
    remote(gath.at[ch], gath.at[ch], ag_send, ag_sem.at[ch], partner)
    gm[2] = (gg[...] * conv).astype(BF16)

    arrive(r_gpre, 4)
    grad_pre = from_pieces(r_gpre) + skip_ref[...] * gc[...]
    gm[0] = (grad_pre * mixed[1].astype(F32)).astype(BF16)
    gm[1] = (grad_pre * mixed[0].astype(F32)).astype(BF16)

    def input_chunk(index):
        span = pl.ds(pl.multiple_of(index * feats, feats), feats)
        total = dot_nt(gm[0], win[0, span, :])
        total += dot_nt(gm[1], win[1, span, :])
        return total + dot_nt(gm[2], win[2, span, :])

    for k in (2, 1, 3, 0):
        to = peer(k)
        b_send[to] = input_chunk(2 * to + 1 - core).astype(BF16)
        remote(b_send.at[to], b_got.at[to], pair_send.at[1], b_sem.at[to], partner)
    b_own[peer(2)] = input_chunk(2 * peer(2) + core)
    fold(b_own, b_got, b_sem, 2)
    for h in (0, 1):
        far(b_own, b_sum, b_fwd, b_f_sem, 1, h)
    for k in (1, 3):
        b_own[peer(k)] = input_chunk(2 * peer(k) + core)
        fold(b_own, b_got, b_sem, k)
    for h in (0, 1):
        plain(b_own, b_sum, b_in, b_i_sem, 1, h)
    give_back(s_gtaps, r_gtaps, 5)
    b_own[x] = input_chunk(2 * x + core)
    fold(b_own, b_got, b_sem, 0)
    for h in (0, 1):
        onward(b_own, b_sum, b_fwd, b_f_sem, b_in, b_i_sem, 1, h)

    for k in (1, 3, 2):
        slot = 2 * peer(k) + core
        wait(gath.at[slot], ag_sem.at[slot])
        remote(gath.at[slot], gath.at[slot], ag_send, ag_sem.at[slot], partner)
    for k in range(chips):
        slot = 2 * peer(k) + 1 - core
        wait(gath.at[slot], ag_sem.at[slot])

    def output_rows(index):
        weights = wout[pl.ds(pl.multiple_of(index * local_ch, local_ch), local_ch), :]
        return dot(gath[index], weights)

    total = output_rows(0)
    for i in range(1, chans):
        total += output_rows(i)
    o_out[...] = total.astype(BF16)
    out_copy = pltpu.make_async_copy(o_out, out_h, store_sem.at[0])
    out_copy.start()

    arrive(r_gtaps, 5)
    o_gtaps[...] = from_pieces(r_gtaps) * scale
    gtaps_copy = pltpu.make_async_copy(o_gtaps, gtaps_h, store_sem.at[1])
    gtaps_copy.start()

    for h in (0, 1):
        o_gtok[:, columns(o_gtok, h)] = collect(b_own, b_in, b_i_sem, h).astype(BF16)
    gtok_copy = pltpu.make_async_copy(o_gtok, gtok_h, store_sem.at[2])
    gtok_copy.start()

    for n, buf in enumerate((s_taps, s_pre, s_grad, s_conv, s_gpre, s_gtaps)):
        wait(buf.at[pl.ds(0, ranks - 1)], seq_send.at[n])
    wait(a_send, pair_send.at[0])
    wait(b_send, pair_send.at[1])
    wait(a_sum, x_send.at[0])
    wait(b_sum, x_send.at[1])
    wait(gath.at[pl.ds(0, 7)], ag_send)
    out_copy.wait()
    gtaps_copy.wait()
    gtok_copy.wait()


def place(a, b, c, d, e, f, sem):
    copies = [
        pltpu.make_async_copy(src, dst, sem.at[i])
        for i, (src, dst) in enumerate(((a, d), (b, e), (c, f)))
    ]
    for copy in copies:
        copy.start()
    for copy in copies:
        copy.wait()


def on_device(ranks, chans, tokens, in_weight, filter_taps, skip_gain, out_weight, grad_out):
    block, width = tokens.shape
    local_ch = in_weight.shape[2]
    feats = grad_out.shape[1]
    per = local_ch // ranks
    chips = chans // 2
    half = 2 * ranks * per
    weight = jnp.transpose(in_weight, (1, 0, 2))
    constants = tables(ranks, per)
    hbm = pl.BlockSpec(memory_space=pl.ANY)
    vmem = pl.BlockSpec(memory_space=pltpu.VMEM)
    piece = (ranks, 2 * per, LANES)
    chunk = (chips, block, local_ch)
    wide = (chips, block, feats)

    def travel(count):
        shapes = (
            (3, 2, block, count // 2),
            (2, 2, block // 2, count // 2),
            (2, 2, block, count // 2),
        )
        return [pltpu.VMEM(shape, BF16) for shape in shapes]

    scratch = [
        pltpu.VMEM(tokens.shape, BF16),
        pltpu.VMEM(weight.shape, BF16),
        pltpu.VMEM(filter_taps.shape, F32),
        pltpu.VMEM(out_weight.shape, BF16),
        pltpu.VMEM(grad_out.shape, BF16),
        pltpu.VMEM((2 * half, half), BF16),
        pltpu.VMEM((half, 2 * half), BF16),
        pltpu.VMEM((2 * LANES, 2 * LANES), BF16),
        pltpu.VMEM((2 * LANES, 2 * LANES), BF16),
        pltpu.VMEM((half, LANES), F32),
        pltpu.VMEM((half, LANES), F32),
        pltpu.VMEM((3, block, local_ch), BF16),
        pltpu.VMEM((block, local_ch), F32),
        pltpu.VMEM((block, local_ch), F32),
        pltpu.VMEM((block, local_ch), F32),
        pltpu.VMEM((half, 2 * LANES), F32),
        pltpu.VMEM((half, 2 * LANES), F32),
        pltpu.VMEM((half, 2 * LANES), F32),
        *[pltpu.VMEM(piece, BF16) for _ in range(12)],
        pltpu.VMEM(chunk, BF16),
        pltpu.VMEM(chunk, BF16),
        pltpu.VMEM(chunk, F32),
        *travel(local_ch),
        pltpu.VMEM((chans, block, local_ch), BF16),
        pltpu.VMEM((3, block, local_ch), BF16),
        pltpu.VMEM(wide, BF16),
        pltpu.VMEM(wide, BF16),
        pltpu.VMEM(wide, F32),
        *travel(feats),
        pltpu.VMEM((block, feats), BF16),
        pltpu.VMEM((block, feats), BF16),
        pltpu.VMEM((block, local_ch), F32),
        pltpu.SemaphoreType.DMA((13,)),
        pltpu.SemaphoreType.DMA((3,)),
        pltpu.SemaphoreType.DMA((6,)),
        pltpu.SemaphoreType.DMA((6,)),
        pltpu.SemaphoreType.DMA((2,)),
        pltpu.SemaphoreType.DMA((chips,)),
        pltpu.SemaphoreType.DMA((chips,)),
        pltpu.SemaphoreType.DMA((2,)),
        pltpu.SemaphoreType.DMA((2, 2)),
        pltpu.SemaphoreType.DMA((2, 2)),
        pltpu.SemaphoreType.DMA((2, 2, 2)),
        pltpu.SemaphoreType.DMA((2, 2, 2)),
        pltpu.SemaphoreType.DMA,
        pltpu.SemaphoreType.DMA((chans,)),
    ]
    results = pl.pallas_call(
        functools.partial(kernel, ranks, chans),
        out_shape=(
            jax.ShapeDtypeStruct((block, feats), BF16),
            jax.ShapeDtypeStruct((block, feats), BF16),
            jax.ShapeDtypeStruct((block, local_ch), F32),
        ),
        in_specs=[hbm, hbm, hbm, vmem, hbm, hbm] + [hbm] * 6,
        out_specs=(hbm, hbm, hbm),
        scratch_shapes=scratch,
        compiler_params=pltpu.CompilerParams(
            collective_id=0, has_side_effects=True, vmem_limit_bytes=58 * 1024 * 1024
        ),
    )(
        tokens, weight, filter_taps, skip_gain.reshape(1, local_ch), out_weight, grad_out,
        *[jnp.asarray(table) for table in constants],
    )
    return pl.pallas_call(
        place,
        out_shape=tuple(jax.ShapeDtypeStruct(r.shape, r.dtype) for r in results),
        in_specs=[vmem] * 3,
        out_specs=(hbm,) * 3,
        scratch_shapes=[pltpu.SemaphoreType.DMA((3,))],
    )(*results)


def solution(mesh):
    placed = (
        P("seq", None),
        P(None, None, "ch"),
        P("seq", "ch"),
        P("ch"),
        P(None, "ch"),
        P("seq", "ch"),
    )
    return jax.shard_map(
        functools.partial(on_device, mesh.shape["seq"], mesh.shape["ch"]),
        mesh=mesh,
        in_specs=placed,
        out_specs=(P("seq", "ch"), P("seq", "ch"), P("seq", "ch")),
        check_vma=False,
    )
```

```python
import functools
import math

import jax
import jax.numpy as jnp
import ml_dtypes
import numpy as np
from jax import lax
from jax.experimental import pallas as pl
from jax.experimental.pallas import tpu as pltpu
from jax.sharding import PartitionSpec as P

MESH = pl.DeviceIdType.MESH
F32 = jnp.float32
BF16 = jnp.bfloat16
LANES = 128


def tables(ranks, per):
    rows = 2 * ranks
    length = rows * LANES
    first = np.arange(rows)
    low = first + 0.25
    angle = 2.0 * np.pi * np.outer(low, first) / rows
    eye = np.eye(per)
    cross = np.concatenate(
        [np.kron(np.cos(angle), eye), np.kron(-np.sin(angle), eye)], axis=0
    )
    cross_back = cross.T / length
    turn = 2.0 * np.pi * np.outer(np.repeat(low, per), np.arange(LANES)) / length
    inner = 2.0 * np.pi * np.outer(np.arange(LANES), np.arange(LANES)) / LANES
    cosine, sine = np.cos(inner), np.sin(inner)
    local = np.block([[cosine, -sine], [sine, cosine]])
    narrow = ml_dtypes.bfloat16
    return (
        cross.astype(narrow),
        cross_back.astype(narrow),
        local.astype(narrow),
        local.T.astype(narrow),
        np.cos(turn).astype(np.float32),
        (-np.sin(turn)).astype(np.float32),
    )


def dot(left, right):
    return jnp.dot(left, right, preferred_element_type=F32)


def dot_nt(left, right):
    return lax.dot_general(
        left, right, (((1,), (1,)), ((), ())), preferred_element_type=F32
    )


def kernel(
    ranks,
    chans,
    *refs,
):
    (
        tok_h, win_h, taps_h, skip_ref, wout_h, gout_h,
        cross_h, back_h, local_h, unlocal_h, tr_h, ti_h,
        out_h, gtok_h, gtaps_h,
        tok, win, taps, wout, gout, cross, back, local, unlocal, tr, ti,
        mixed, pre, gg, gc, spec_t, spec_p, spec_g,
        s_taps, s_pre, s_grad, s_conv, s_gpre, s_gtaps,
        r_taps, r_pre, r_grad, r_conv, r_gpre, r_gtaps,
        a_send, a_got, a_own, a_sum, a_fwd, a_in,
        gath, gm,
        b_send, b_got, b_own, b_sum, b_fwd, b_in,
        o_out, o_gtok, o_gtaps,
        load_sem, store_sem, seq_send, seq_recv,
        pair_send, a_sem, b_sem, x_send, a_f_sem, b_f_sem, a_i_sem, b_i_sem,
        ag_send, ag_sem,
    ) = refs
    seq = lax.axis_index("seq")
    ch = lax.axis_index("ch")
    chips = chans // 2
    x, core = lax.div(ch, 2), lax.rem(ch, 2)
    partner = (seq, ch + 1 - 2 * core)
    block, width = tok.shape
    local_ch = win.shape[2]
    per = local_ch // ranks
    feats = gout.shape[1]
    half = ranks * 2 * per
    scale = (ranks * block) ** -0.5
    part = block // 2
    turns = 4 if ranks % 8 == 0 else 1
    some = ranks // 2

    def peer(step):
        return lax.rem(x + step, chips)

    def slot_of(rank):
        z, y = lax.div(rank, turns), lax.rem(rank, turns)
        return lax.rem(z, 2) * some + lax.div(z, 2) * turns + y

    def rank_of(slot):
        side, rest = lax.div(slot, some), lax.rem(slot, some)
        return (2 * lax.div(rest, turns) + side) * turns + lax.rem(rest, turns)

    mine = slot_of(seq)

    loads = [
        (taps_h, taps), (gout_h, gout), (wout_h, wout), (tok_h, tok),
        (win_h.at[0], win.at[0]), (win_h.at[1], win.at[1]), (win_h.at[2], win.at[2]),
        (cross_h, cross), (local_h, local), (tr_h, tr), (ti_h, ti),
        (unlocal_h, unlocal), (back_h, back),
    ]
    copies = [
        pltpu.make_async_copy(src, dst, load_sem.at[i])
        for i, (src, dst) in enumerate(loads)
    ]
    for copy in copies[:3]:
        copy.start()

    barrier = pltpu.get_barrier_semaphore()

    def greet(k, carry):
        pl.semaphore_signal(
            barrier, inc=1, device_id=(lax.rem(seq + k, ranks), ch), device_id_type=MESH
        )
        return carry

    lax.fori_loop(1, ranks, greet, 0)
    pl.semaphore_signal(barrier, inc=1, device_id=partner, device_id_type=MESH)
    for k in (1, 2, 3):
        pl.semaphore_signal(
            barrier, inc=1, device_id=(seq, 2 * peer(k) + core), device_id_type=MESH
        )

    def remote(src, dst, send, recv, device):
        copy = pltpu.make_async_remote_copy(
            src_ref=src, dst_ref=dst, send_sem=send, recv_sem=recv,
            device_id=device, device_id_type=MESH,
        )
        copy.start()

    def wait(ref, sem):
        pltpu.make_async_copy(ref, ref, sem).wait()

    def rounds(send):
        first = ranks * 3 // 8
        lax.fori_loop(max(first, 1), ranks, send, 0, unroll=True)
        lax.fori_loop(1, first, send, 0, unroll=True)

    def spread(buf, got, n):
        def send(k, carry):
            to = lax.rem(seq + k, ranks)
            remote(
                buf.at[slot_of(to)], got.at[seq], seq_send.at[n], seq_recv.at[n], (to, ch)
            )
            return carry

        rounds(send)
        got[seq] = buf[mine]

    def spread_side(buf, got, n, side):
        def send(k, carry):
            slot = side * some + lax.rem(mine + k, some)
            to = rank_of(slot)

            @pl.when(to != seq)
            def _():
                remote(
                    buf.at[slot], got.at[seq], seq_send.at[n], seq_recv.at[n], (to, ch)
                )

            return carry

        lax.fori_loop(0, some, send, 0, unroll=True)

    def give_back(buf, got, n):
        def send(k, carry):
            to = lax.rem(seq + k, ranks)
            remote(buf.at[to], got.at[mine], seq_send.at[n], seq_recv.at[n], (to, ch))
            return carry

        rounds(send)
        got[mine] = buf[seq]

    def arrive(got, n):
        wait(got.at[pl.ds(0, ranks - 1)], seq_recv.at[n])

    def to_pieces(value, buf, first):
        turned = value.T
        count = turned.shape[0] // per
        parts = [
            turned[:, i * LANES : (i + 1) * LANES].reshape(count, per, LANES)
            for i in range(2)
        ]
        buf[first : first + count] = jnp.concatenate(parts, axis=1).astype(BF16)

    def from_pieces(got):
        parts = got[...].astype(F32)
        turned = jnp.concatenate(
            [
                parts[:, i * per : (i + 1) * per, :].reshape(local_ch, LANES)
                for i in range(2)
            ],
            axis=1,
        )
        return turned.T

    def spectrum(got):
        flat = got[...].reshape(half, LANES)
        both = dot(cross[...], flat)
        re, im = both[:half], both[half:]
        cosine, sine = tr[...], ti[...]
        turned = jnp.concatenate(
            [re * cosine - im * sine, re * sine + im * cosine], axis=1
        )
        return dot(turned.astype(BF16), local[...])

    def inverse(re, im, buf):
        both = dot(jnp.concatenate([re, im], axis=1).astype(BF16), unlocal[...])
        re, im = both[:, :LANES], both[:, LANES:]
        cosine, sine = tr[...], ti[...]
        turned = jnp.concatenate(
            [re * cosine + im * sine, im * cosine - re * sine], axis=0
        )
        result = dot(back[...], turned.astype(BF16))
        buf[...] = result.astype(BF16).reshape(ranks, 2 * per, LANES)

    near = (1, 3)

    def rows(d):
        return pl.ds(d * part, part)

    def columns(ref, h):
        count = ref.shape[-1] // 2
        return slice(h * count, (h + 1) * count)

    def fold(own, got, sem, k):
        to = peer(k)
        wait(got.at[to], sem.at[to])
        own[to] = own[to] + got[to].astype(F32)

    def far(own, sums, fwd, f_sem, n, h):
        sums[0, h] = own[peer(2), :, columns(own, h)].astype(BF16)
        for d in (0, 1):
            remote(
                sums.at[0, h, rows(d)], fwd.at[d, h], x_send.at[n], f_sem.at[d, h],
                (seq, 2 * peer(near[d]) + core),
            )

    def plain(own, sums, into, i_sem, n, h):
        for d in (0, 1):
            to = peer(near[d])
            sums[1 + d, h, rows(1 - d)] = own[
                to, rows(1 - d), columns(own, h)
            ].astype(BF16)
            remote(
                sums.at[1 + d, h, rows(1 - d)], into.at[d, h, rows(1 - d)],
                x_send.at[n], i_sem.at[0, d, h], (seq, 2 * to + core),
            )

    def onward(own, sums, fwd, f_sem, into, i_sem, n, h):
        for d in (0, 1):
            to = peer(near[d])
            wait(fwd.at[d, h], f_sem.at[d, h])
            sums[1 + d, h, rows(d)] = (
                own[to, rows(d), columns(own, h)] + fwd[d, h].astype(F32)
            ).astype(BF16)
            remote(
                sums.at[1 + d, h, rows(d)], into.at[d, h, rows(d)],
                x_send.at[n], i_sem.at[1, d, h], (seq, 2 * to + core),
            )

    def collect(own, into, i_sem, h):
        for d in (0, 1):
            wait(into.at[d, h, rows(1 - d)], i_sem.at[0, d, h])
            wait(into.at[d, h, rows(d)], i_sem.at[1, d, h])
        return own[x, :, columns(own, h)] + (
            into[0, h].astype(F32) + into[1, h].astype(F32)
        )

    def feature_chunk(index):
        weights = wout[pl.ds(pl.multiple_of(index * local_ch, local_ch), local_ch), :]
        return dot_nt(gout[...], weights)

    copies[0].wait()
    for copy in copies[3:]:
        copy.start()
    to_pieces(taps[...] * scale, s_taps, 0)
    copies[1].wait()
    copies[2].wait()
    for k in (2, 1, 3, 0):
        to = peer(k)
        a_send[to] = feature_chunk(2 * to + 1 - core).astype(BF16)
    pl.semaphore_wait(barrier, ranks - 1 + 1 + 3)
    for k in (2, 1, 3, 0):
        to = peer(k)
        remote(a_send.at[to], a_got.at[to], pair_send.at[0], a_sem.at[to], partner)
    spread(s_taps, r_taps, 0)
    for k in (2, 1, 3, 0):
        to = peer(k)
        a_own[to] = feature_chunk(2 * to + core)
    fold(a_own, a_got, a_sem, 2)
    far(a_own, a_sum, a_fwd, a_f_sem, 0, 0)
    far(a_own, a_sum, a_fwd, a_f_sem, 0, 1)

    copies[3].wait()
    copies[4].wait()
    mixed[0] = dot(tok[...], win[0]).astype(BF16)
    fold(a_own, a_got, a_sem, 1)
    fold(a_own, a_got, a_sem, 3)
    plain(a_own, a_sum, a_in, a_i_sem, 0, 0)
    plain(a_own, a_sum, a_in, a_i_sem, 0, 1)
    copies[5].wait()
    mixed[1] = dot(tok[...], win[1]).astype(BF16)
    pre[...] = mixed[1].astype(F32) * mixed[0].astype(F32)
    to_pieces(pre[...], s_pre, 0)
    spread(s_pre, r_pre, 1)
    onward(a_own, a_sum, a_fwd, a_f_sem, a_in, a_i_sem, 0, 0)
    onward(a_own, a_sum, a_fwd, a_f_sem, a_in, a_i_sem, 0, 1)
    fold(a_own, a_got, a_sem, 0)
    copies[6].wait()
    mixed[2] = dot(tok[...], win[2]).astype(BF16)

    for h in (0, 1):
        cut = columns(gg, h)
        gg[:, cut] = collect(a_own, a_in, a_i_sem, h)
        gc[:, cut] = gg[:, cut] * mixed[2, :, cut].astype(F32)
        to_pieces(gc[:, cut], s_grad, h * some)
        spread_side(s_grad, r_grad, 2, h)
    r_grad[seq] = s_grad[mine]

    for copy in copies[7:]:
        copy.wait()
    arrive(r_taps, 0)
    spec_t[...] = spectrum(r_taps)
    arrive(r_pre, 1)
    spec_p[...] = spectrum(r_pre)
    t_re, t_im = spec_t[:, :LANES], spec_t[:, LANES:]
    p_re, p_im = spec_p[:, :LANES], spec_p[:, LANES:]
    inverse(t_re * p_re - t_im * p_im, t_re * p_im + t_im * p_re, s_conv)
    give_back(s_conv, r_conv, 3)
    arrive(r_grad, 2)
    spec_g[...] = spectrum(r_grad)
    g_re, g_im = spec_g[:, :LANES], spec_g[:, LANES:]
    t_re, t_im = spec_t[:, :LANES], spec_t[:, LANES:]
    inverse(t_re * g_re + t_im * g_im, t_re * g_im - t_im * g_re, s_gpre)
    give_back(s_gpre, r_gpre, 4)
    p_re, p_im = spec_p[:, :LANES], spec_p[:, LANES:]
    g_re, g_im = spec_g[:, :LANES], spec_g[:, LANES:]
    inverse(p_re * g_re + p_im * g_im, p_re * g_im - p_im * g_re, s_gtaps)

    arrive(r_conv, 3)
    conv = from_pieces(r_conv) + skip_ref[...] * pre[...]
    gath[ch] = (mixed[2].astype(F32) * conv).astype(BF16)
    for k in (2, 1, 3):
        remote(
            gath.at[ch], gath.at[ch], ag_send, ag_sem.at[ch], (seq, 2 * peer(k) + core)
        )
    remote(gath.at[ch], gath.at[ch], ag_send, ag_sem.at[ch], partner)
    gm[2] = (gg[...] * conv).astype(BF16)

    arrive(r_gpre, 4)
    grad_pre = from_pieces(r_gpre) + skip_ref[...] * gc[...]
    gm[0] = (grad_pre * mixed[1].astype(F32)).astype(BF16)
    gm[1] = (grad_pre * mixed[0].astype(F32)).astype(BF16)

    def input_chunk(index):
        span = pl.ds(pl.multiple_of(index * feats, feats), feats)
        total = dot_nt(gm[0], win[0, span, :])
        total += dot_nt(gm[1], win[1, span, :])
        return total + dot_nt(gm[2], win[2, span, :])

    def to_partner(k):
        to = peer(k)
        b_send[to] = input_chunk(2 * to + 1 - core).astype(BF16)
        remote(b_send.at[to], b_got.at[to], pair_send.at[1], b_sem.at[to], partner)

    def to_self(k):
        b_own[peer(k)] = input_chunk(2 * peer(k) + core)

    to_partner(2)
    to_self(2)
    fold(b_own, b_got, b_sem, 2)
    for h in (0, 1):
        far(b_own, b_sum, b_fwd, b_f_sem, 1, h)
    to_partner(1)
    to_partner(3)
    give_back(s_gtaps, r_gtaps, 5)
    to_self(1)
    to_self(3)
    fold(b_own, b_got, b_sem, 1)
    fold(b_own, b_got, b_sem, 3)
    for h in (0, 1):
        plain(b_own, b_sum, b_in, b_i_sem, 1, h)
    to_partner(0)
    for h in (0, 1):
        onward(b_own, b_sum, b_fwd, b_f_sem, b_in, b_i_sem, 1, h)
    to_self(0)
    fold(b_own, b_got, b_sem, 0)

    for k in (1, 3, 2):
        slot = 2 * peer(k) + core
        wait(gath.at[slot], ag_sem.at[slot])
        remote(gath.at[slot], gath.at[slot], ag_send, ag_sem.at[slot], partner)
    for k in range(chips):
        slot = 2 * peer(k) + 1 - core
        wait(gath.at[slot], ag_sem.at[slot])

    def output_rows(index):
        weights = wout[pl.ds(pl.multiple_of(index * local_ch, local_ch), local_ch), :]
        return dot(gath[index], weights)

    total = output_rows(0)
    for i in range(1, chans):
        total += output_rows(i)
    o_out[...] = total.astype(BF16)
    out_copy = pltpu.make_async_copy(o_out, out_h, store_sem.at[0])
    out_copy.start()

    arrive(r_gtaps, 5)
    o_gtaps[...] = from_pieces(r_gtaps) * scale
    gtaps_copy = pltpu.make_async_copy(o_gtaps, gtaps_h, store_sem.at[1])
    gtaps_copy.start()

    for h in (0, 1):
        o_gtok[:, columns(o_gtok, h)] = collect(b_own, b_in, b_i_sem, h).astype(BF16)
    gtok_copy = pltpu.make_async_copy(o_gtok, gtok_h, store_sem.at[2])
    gtok_copy.start()

    for n, buf in enumerate((s_taps, s_pre, s_grad, s_conv, s_gpre, s_gtaps)):
        wait(buf.at[pl.ds(0, ranks - 1)], seq_send.at[n])
    wait(a_send, pair_send.at[0])
    wait(b_send, pair_send.at[1])
    wait(a_sum, x_send.at[0])
    wait(b_sum, x_send.at[1])
    wait(gath.at[pl.ds(0, 7)], ag_send)
    out_copy.wait()
    gtaps_copy.wait()
    gtok_copy.wait()


def place(a, b, c, d, e, f, sem):
    copies = [
        pltpu.make_async_copy(src, dst, sem.at[i])
        for i, (src, dst) in enumerate(((a, d), (b, e), (c, f)))
    ]
    for copy in copies:
        copy.start()
    for copy in copies:
        copy.wait()


def on_device(ranks, chans, tokens, in_weight, filter_taps, skip_gain, out_weight, grad_out):
    block, width = tokens.shape
    local_ch = in_weight.shape[2]
    feats = grad_out.shape[1]
    per = local_ch // ranks
    chips = chans // 2
    half = 2 * ranks * per
    weight = jnp.transpose(in_weight, (1, 0, 2))
    constants = tables(ranks, per)
    hbm = pl.BlockSpec(memory_space=pl.ANY)
    vmem = pl.BlockSpec(memory_space=pltpu.VMEM)
    piece = (ranks, 2 * per, LANES)
    chunk = (chips, block, local_ch)
    wide = (chips, block, feats)

    def travel(count):
        shapes = (
            (3, 2, block, count // 2),
            (2, 2, block // 2, count // 2),
            (2, 2, block, count // 2),
        )
        return [pltpu.VMEM(shape, BF16) for shape in shapes]

    scratch = [
        pltpu.VMEM(tokens.shape, BF16),
        pltpu.VMEM(weight.shape, BF16),
        pltpu.VMEM(filter_taps.shape, F32),
        pltpu.VMEM(out_weight.shape, BF16),
        pltpu.VMEM(grad_out.shape, BF16),
        pltpu.VMEM((2 * half, half), BF16),
        pltpu.VMEM((half, 2 * half), BF16),
        pltpu.VMEM((2 * LANES, 2 * LANES), BF16),
        pltpu.VMEM((2 * LANES, 2 * LANES), BF16),
        pltpu.VMEM((half, LANES), F32),
        pltpu.VMEM((half, LANES), F32),
        pltpu.VMEM((3, block, local_ch), BF16),
        pltpu.VMEM((block, local_ch), F32),
        pltpu.VMEM((block, local_ch), F32),
        pltpu.VMEM((block, local_ch), F32),
        pltpu.VMEM((half, 2 * LANES), F32),
        pltpu.VMEM((half, 2 * LANES), F32),
        pltpu.VMEM((half, 2 * LANES), F32),
        *[pltpu.VMEM(piece, BF16) for _ in range(12)],
        pltpu.VMEM(chunk, BF16),
        pltpu.VMEM(chunk, BF16),
        pltpu.VMEM(chunk, F32),
        *travel(local_ch),
        pltpu.VMEM((chans, block, local_ch), BF16),
        pltpu.VMEM((3, block, local_ch), BF16),
        pltpu.VMEM(wide, BF16),
        pltpu.VMEM(wide, BF16),
        pltpu.VMEM(wide, F32),
        *travel(feats),
        pltpu.VMEM((block, feats), BF16),
        pltpu.VMEM((block, feats), BF16),
        pltpu.VMEM((block, local_ch), F32),
        pltpu.SemaphoreType.DMA((13,)),
        pltpu.SemaphoreType.DMA((3,)),
        pltpu.SemaphoreType.DMA((6,)),
        pltpu.SemaphoreType.DMA((6,)),
        pltpu.SemaphoreType.DMA((2,)),
        pltpu.SemaphoreType.DMA((chips,)),
        pltpu.SemaphoreType.DMA((chips,)),
        pltpu.SemaphoreType.DMA((2,)),
        pltpu.SemaphoreType.DMA((2, 2)),
        pltpu.SemaphoreType.DMA((2, 2)),
        pltpu.SemaphoreType.DMA((2, 2, 2)),
        pltpu.SemaphoreType.DMA((2, 2, 2)),
        pltpu.SemaphoreType.DMA,
        pltpu.SemaphoreType.DMA((chans,)),
    ]
    results = pl.pallas_call(
        functools.partial(kernel, ranks, chans),
        out_shape=(
            jax.ShapeDtypeStruct((block, feats), BF16),
            jax.ShapeDtypeStruct((block, feats), BF16),
            jax.ShapeDtypeStruct((block, local_ch), F32),
        ),
        in_specs=[hbm, hbm, hbm, vmem, hbm, hbm] + [hbm] * 6,
        out_specs=(hbm, hbm, hbm),
        scratch_shapes=scratch,
        compiler_params=pltpu.CompilerParams(
            collective_id=0, has_side_effects=True, vmem_limit_bytes=58 * 1024 * 1024
        ),
    )(
        tokens, weight, filter_taps, skip_gain.reshape(1, local_ch), out_weight, grad_out,
        *[jnp.asarray(table) for table in constants],
    )
    return pl.pallas_call(
        place,
        out_shape=tuple(jax.ShapeDtypeStruct(r.shape, r.dtype) for r in results),
        in_specs=[vmem] * 3,
        out_specs=(hbm,) * 3,
        scratch_shapes=[pltpu.SemaphoreType.DMA((3,))],
    )(*results)


def solution(mesh):
    placed = (
        P("seq", None),
        P(None, None, "ch"),
        P("seq", "ch"),
        P("ch"),
        P(None, "ch"),
        P("seq", "ch"),
    )
    return jax.shard_map(
        functools.partial(on_device, mesh.shape["seq"], mesh.shape["ch"]),
        mesh=mesh,
        in_specs=placed,
        out_specs=(P("seq", "ch"), P("seq", "ch"), P("seq", "ch")),
        check_vma=False,
    )
```

```python
import functools
import math

import jax
import jax.numpy as jnp
import ml_dtypes
import numpy as np
from jax import lax
from jax.experimental import pallas as pl
from jax.experimental.pallas import tpu as pltpu
from jax.sharding import PartitionSpec as P

MESH = pl.DeviceIdType.MESH
F32 = jnp.float32
BF16 = jnp.bfloat16
LANES = 128


def tables(ranks, per):
    rows = 2 * ranks
    length = rows * LANES
    first = np.arange(rows)
    low = first + 0.25
    angle = 2.0 * np.pi * np.outer(low, first) / rows
    eye = np.eye(per)
    cross = np.concatenate(
        [np.kron(np.cos(angle), eye), np.kron(-np.sin(angle), eye)], axis=0
    )
    cross_back = cross.T / length
    turn = 2.0 * np.pi * np.outer(np.repeat(low, per), np.arange(LANES)) / length
    inner = 2.0 * np.pi * np.outer(np.arange(LANES), np.arange(LANES)) / LANES
    cosine, sine = np.cos(inner), np.sin(inner)
    local = np.block([[cosine, -sine], [sine, cosine]])
    narrow = ml_dtypes.bfloat16
    return (
        cross.astype(narrow),
        cross_back.astype(narrow),
        local.astype(narrow),
        local.T.astype(narrow),
        np.cos(turn).astype(np.float32),
        (-np.sin(turn)).astype(np.float32),
    )


def dot(left, right):
    return jnp.dot(left, right, preferred_element_type=F32)


def dot_nt(left, right):
    return lax.dot_general(
        left, right, (((1,), (1,)), ((), ())), preferred_element_type=F32
    )


def kernel(
    ranks,
    chans,
    *refs,
):
    (
        tok_h, win_h, taps_h, skip_ref, wout_h, gout_h,
        cross_h, back_h, local_h, unlocal_h, tr_h, ti_h,
        out_h, gtok_h, gtaps_h,
        tok, win, taps, wout, gout, cross, back, local, unlocal, tr, ti,
        mixed, pre, gg, gc, spec_t, spec_p, spec_g, early,
        s_taps, s_pre, s_grad, s_conv, s_gpre, s_gtaps,
        r_taps, r_pre, r_grad, r_conv, r_gpre, r_gtaps,
        a_send, a_got, a_own, a_sum, a_fwd, a_in,
        gath, gm,
        b_send, b_got, b_own, b_sum, b_fwd, b_in,
        o_out, o_gtok, o_gtaps,
        load_sem, store_sem, seq_send, seq_recv,
        pair_send, a_sem, b_sem, x_send, a_f_sem, b_f_sem, a_i_sem, b_i_sem,
        ag_send, ag_sem,
    ) = refs
    seq = lax.axis_index("seq")
    ch = lax.axis_index("ch")
    chips = chans // 2
    x, core = lax.div(ch, 2), lax.rem(ch, 2)
    partner = (seq, ch + 1 - 2 * core)
    block, width = tok.shape
    local_ch = win.shape[2]
    per = local_ch // ranks
    feats = gout.shape[1]
    half = ranks * 2 * per
    scale = (ranks * block) ** -0.5
    part = block // 2
    turns = 4 if ranks % 8 == 0 else 1
    some = ranks // 2

    def peer(step):
        return lax.rem(x + step, chips)

    def slot_of(rank):
        z, y = lax.div(rank, turns), lax.rem(rank, turns)
        return lax.rem(z, 2) * some + lax.div(z, 2) * turns + y

    def rank_of(slot):
        side, rest = lax.div(slot, some), lax.rem(slot, some)
        return (2 * lax.div(rest, turns) + side) * turns + lax.rem(rest, turns)

    mine = slot_of(seq)

    def rounds(send):
        first = ranks * 3 // 8
        lax.fori_loop(max(first, 1), ranks, send, 0, unroll=True)
        lax.fori_loop(1, first, send, 0, unroll=True)

    barrier = pltpu.get_barrier_semaphore()

    def greet(k, carry):
        pl.semaphore_signal(
            barrier, inc=1, device_id=(lax.rem(seq + k, ranks), ch), device_id_type=MESH
        )
        return carry

    rounds(greet)
    pl.semaphore_signal(barrier, inc=1, device_id=partner, device_id_type=MESH)
    for k in (1, 2, 3):
        pl.semaphore_signal(
            barrier, inc=1, device_id=(seq, 2 * peer(k) + core), device_id_type=MESH
        )

    loads = [
        (taps_h, taps), (gout_h, gout), (wout_h, wout), (tok_h, tok),
        (win_h.at[0], win.at[0]), (win_h.at[1], win.at[1]), (win_h.at[2], win.at[2]),
        (cross_h, cross), (local_h, local), (tr_h, tr), (ti_h, ti),
        (unlocal_h, unlocal), (back_h, back),
    ]
    copies = [
        pltpu.make_async_copy(src, dst, load_sem.at[i])
        for i, (src, dst) in enumerate(loads)
    ]
    for copy in copies[:3]:
        copy.start()

    def remote(src, dst, send, recv, device):
        copy = pltpu.make_async_remote_copy(
            src_ref=src, dst_ref=dst, send_sem=send, recv_sem=recv,
            device_id=device, device_id_type=MESH,
        )
        copy.start()

    def wait(ref, sem):
        pltpu.make_async_copy(ref, ref, sem).wait()

    def spread(buf, got, n):
        def send(k, carry):
            to = lax.rem(seq + k, ranks)
            remote(
                buf.at[slot_of(to)], got.at[seq], seq_send.at[n], seq_recv.at[n], (to, ch)
            )
            return carry

        rounds(send)
        got[seq] = buf[mine]

    def spread_side(buf, got, n, side):
        def send(k, carry):
            slot = side * some + lax.rem(mine + some * 3 // 8 + k, some)
            to = rank_of(slot)

            @pl.when(to != seq)
            def _():
                remote(
                    buf.at[slot], got.at[seq], seq_send.at[n], seq_recv.at[n], (to, ch)
                )

            return carry

        lax.fori_loop(0, some, send, 0, unroll=True)

    def give_back(buf, got, n):
        def send(k, carry):
            to = lax.rem(seq + k, ranks)
            remote(buf.at[to], got.at[mine], seq_send.at[n], seq_recv.at[n], (to, ch))
            return carry

        rounds(send)
        got[mine] = buf[seq]

    def arrive(got, n):
        wait(got.at[pl.ds(0, ranks - 1)], seq_recv.at[n])

    def to_pieces(value, buf, first):
        turned = value.T
        count = turned.shape[0] // per
        parts = [
            turned[:, i * LANES : (i + 1) * LANES].reshape(count, per, LANES)
            for i in range(2)
        ]
        buf[first : first + count] = jnp.concatenate(parts, axis=1).astype(BF16)

    def from_pieces(got):
        parts = got[...].astype(F32)
        turned = jnp.concatenate(
            [
                parts[:, i * per : (i + 1) * per, :].reshape(local_ch, LANES)
                for i in range(2)
            ],
            axis=1,
        )
        return turned.T

    def spectrum(got):
        flat = got[...].reshape(half, LANES)
        both = dot(cross[...], flat)
        re, im = both[:half], both[half:]
        cosine, sine = tr[...], ti[...]
        turned = jnp.concatenate(
            [re * cosine - im * sine, re * sine + im * cosine], axis=1
        )
        return dot(turned.astype(BF16), local[...])

    def inverse(re, im, buf):
        both = dot(jnp.concatenate([re, im], axis=1).astype(BF16), unlocal[...])
        re, im = both[:, :LANES], both[:, LANES:]
        cosine, sine = tr[...], ti[...]
        turned = jnp.concatenate(
            [re * cosine + im * sine, im * cosine - re * sine], axis=0
        )
        result = dot(back[...], turned.astype(BF16))
        buf[...] = result.astype(BF16).reshape(ranks, 2 * per, LANES)

    near = (1, 3)

    def rows(d):
        return pl.ds(d * part, part)

    def columns(ref, h):
        count = ref.shape[-1] // 2
        return slice(h * count, (h + 1) * count)

    def fold(own, got, sem, k):
        to = peer(k)
        wait(got.at[to], sem.at[to])
        own[to] = own[to] + got[to].astype(F32)

    def far(own, sums, fwd, f_sem, n, h):
        sums[0, h] = own[peer(2), :, columns(own, h)].astype(BF16)
        for d in (0, 1):
            remote(
                sums.at[0, h, rows(d)], fwd.at[d, h], x_send.at[n], f_sem.at[d, h],
                (seq, 2 * peer(near[d]) + core),
            )

    def plain(own, sums, into, i_sem, n, h):
        for d in (0, 1):
            to = peer(near[d])
            sums[1 + d, h, rows(1 - d)] = own[
                to, rows(1 - d), columns(own, h)
            ].astype(BF16)
            remote(
                sums.at[1 + d, h, rows(1 - d)], into.at[d, h, rows(1 - d)],
                x_send.at[n], i_sem.at[0, d, h], (seq, 2 * to + core),
            )

    def onward(own, sums, fwd, f_sem, into, i_sem, n, h):
        for d in (0, 1):
            to = peer(near[d])
            wait(fwd.at[d, h], f_sem.at[d, h])
            sums[1 + d, h, rows(d)] = (
                own[to, rows(d), columns(own, h)] + fwd[d, h].astype(F32)
            ).astype(BF16)
            remote(
                sums.at[1 + d, h, rows(d)], into.at[d, h, rows(d)],
                x_send.at[n], i_sem.at[1, d, h], (seq, 2 * to + core),
            )

    def collect(own, into, i_sem, h):
        for d in (0, 1):
            wait(into.at[d, h, rows(1 - d)], i_sem.at[0, d, h])
            wait(into.at[d, h, rows(d)], i_sem.at[1, d, h])
        return own[x, :, columns(own, h)] + (
            into[0, h].astype(F32) + into[1, h].astype(F32)
        )

    def feature_chunk(index):
        weights = wout[pl.ds(pl.multiple_of(index * local_ch, local_ch), local_ch), :]
        return dot_nt(gout[...], weights)

    copies[0].wait()
    for copy in copies[3:]:
        copy.start()
    to_pieces(taps[...] * scale, s_taps, 0)
    copies[1].wait()
    copies[2].wait()
    for k in (2, 1, 3, 0):
        to = peer(k)
        a_send[to] = feature_chunk(2 * to + 1 - core).astype(BF16)
    pl.semaphore_wait(barrier, ranks - 1 + 1 + 3)
    for k in (2, 1, 3, 0):
        to = peer(k)
        remote(a_send.at[to], a_got.at[to], pair_send.at[0], a_sem.at[to], partner)
    spread(s_taps, r_taps, 0)
    for k in (2, 1, 3, 0):
        to = peer(k)
        a_own[to] = feature_chunk(2 * to + core)
    fold(a_own, a_got, a_sem, 2)
    far(a_own, a_sum, a_fwd, a_f_sem, 0, 0)
    far(a_own, a_sum, a_fwd, a_f_sem, 0, 1)

    copies[3].wait()
    copies[4].wait()
    mixed[0] = dot(tok[...], win[0]).astype(BF16)
    fold(a_own, a_got, a_sem, 1)
    fold(a_own, a_got, a_sem, 3)
    plain(a_own, a_sum, a_in, a_i_sem, 0, 0)
    plain(a_own, a_sum, a_in, a_i_sem, 0, 1)
    copies[5].wait()
    mixed[1] = dot(tok[...], win[1]).astype(BF16)
    pre[...] = mixed[1].astype(F32) * mixed[0].astype(F32)
    to_pieces(pre[...], s_pre, 0)
    spread(s_pre, r_pre, 1)
    onward(a_own, a_sum, a_fwd, a_f_sem, a_in, a_i_sem, 0, 0)
    onward(a_own, a_sum, a_fwd, a_f_sem, a_in, a_i_sem, 0, 1)
    fold(a_own, a_got, a_sem, 0)
    copies[6].wait()
    mixed[2] = dot(tok[...], win[2]).astype(BF16)

    for h in (0, 1):
        cut = columns(gg, h)
        gg[:, cut] = collect(a_own, a_in, a_i_sem, h)
        gc[:, cut] = gg[:, cut] * mixed[2, :, cut].astype(F32)
        to_pieces(gc[:, cut], s_grad, h * some)
        spread_side(s_grad, r_grad, 2, h)
    r_grad[seq] = s_grad[mine]

    for copy in copies[7:]:
        copy.wait()
    arrive(r_taps, 0)
    spec_t[...] = spectrum(r_taps)
    arrive(r_pre, 1)
    spec_p[...] = spectrum(r_pre)
    t_re, t_im = spec_t[:, :LANES], spec_t[:, LANES:]
    p_re, p_im = spec_p[:, :LANES], spec_p[:, LANES:]
    inverse(t_re * p_re - t_im * p_im, t_re * p_im + t_im * p_re, s_conv)
    give_back(s_conv, r_conv, 3)
    arrive(r_grad, 2)
    spec_g[...] = spectrum(r_grad)
    g_re, g_im = spec_g[:, :LANES], spec_g[:, LANES:]
    t_re, t_im = spec_t[:, :LANES], spec_t[:, LANES:]
    inverse(t_re * g_re + t_im * g_im, t_re * g_im - t_im * g_re, s_gpre)
    give_back(s_gpre, r_gpre, 4)
    p_re, p_im = spec_p[:, :LANES], spec_p[:, LANES:]
    g_re, g_im = spec_g[:, :LANES], spec_g[:, LANES:]
    inverse(p_re * g_re + p_im * g_im, p_re * g_im - p_im * g_re, s_gtaps)

    arrive(r_conv, 3)
    conv = from_pieces(r_conv) + skip_ref[...] * pre[...]
    gath[ch] = (mixed[2].astype(F32) * conv).astype(BF16)
    for k in (2, 1, 3):
        remote(
            gath.at[ch], gath.at[ch], ag_send, ag_sem.at[ch], (seq, 2 * peer(k) + core)
        )
    remote(gath.at[ch], gath.at[ch], ag_send, ag_sem.at[ch], partner)
    gm[2] = (gg[...] * conv).astype(BF16)
    for i in (0, 1):
        owner = 2 * peer(2) + (core if i else 1 - core)
        span = pl.ds(pl.multiple_of(owner * feats, feats), feats)
        early[i] = dot_nt(gm[2], win[2, span, :])

    arrive(r_gpre, 4)
    grad_pre = from_pieces(r_gpre) + skip_ref[...] * gc[...]
    gm[0] = (grad_pre * mixed[1].astype(F32)).astype(BF16)
    gm[1] = (grad_pre * mixed[0].astype(F32)).astype(BF16)

    def input_chunk(index):
        span = pl.ds(pl.multiple_of(index * feats, feats), feats)
        total = dot_nt(gm[0], win[0, span, :])
        total += dot_nt(gm[1], win[1, span, :])
        return total + dot_nt(gm[2], win[2, span, :])

    def to_partner(k):
        to = peer(k)
        b_send[to] = input_chunk(2 * to + 1 - core).astype(BF16)
        remote(b_send.at[to], b_got.at[to], pair_send.at[1], b_sem.at[to], partner)

    def to_self(k):
        b_own[peer(k)] = input_chunk(2 * peer(k) + core)

    def half_chunk(i, h):
        owner = 2 * peer(2) + (core if i else 1 - core)
        count = feats // 2
        span = pl.ds(pl.multiple_of(owner * feats + h * count, count), count)
        total = early[i, :, columns(early, h)] + dot_nt(gm[0], win[0, span, :])
        return total + dot_nt(gm[1], win[1, span, :])

    to = peer(2)
    pair_sem = (b_sem.at[to], b_sem.at[chips])

    def half_to_partner(h):
        cut = columns(b_send, h)
        b_send[to, :, cut] = half_chunk(0, h).astype(BF16)
        remote(
            b_send.at[to, :, cut], b_got.at[to, :, cut], pair_send.at[1], pair_sem[h],
            partner,
        )

    def half_far(h):
        cut = columns(b_own, h)
        wait(b_got.at[to, :, cut], pair_sem[h])
        b_own[to, :, cut] = b_own[to, :, cut] + b_got[to, :, cut].astype(F32)
        far(b_own, b_sum, b_fwd, b_f_sem, 1, h)

    half_to_partner(0)
    b_own[to, :, columns(b_own, 0)] = half_chunk(1, 0)
    half_to_partner(1)
    half_far(0)
    b_own[to, :, columns(b_own, 1)] = half_chunk(1, 1)
    half_far(1)
    to_partner(1)
    to_partner(3)
    give_back(s_gtaps, r_gtaps, 5)
    to_self(1)
    to_self(3)
    fold(b_own, b_got, b_sem, 1)
    fold(b_own, b_got, b_sem, 3)
    for h in (0, 1):
        plain(b_own, b_sum, b_in, b_i_sem, 1, h)
    to_partner(0)
    onward(b_own, b_sum, b_fwd, b_f_sem, b_in, b_i_sem, 1, 0)
    to_self(0)
    fold(b_own, b_got, b_sem, 0)
    onward(b_own, b_sum, b_fwd, b_f_sem, b_in, b_i_sem, 1, 1)

    for k in (1, 3, 2):
        slot = 2 * peer(k) + core
        wait(gath.at[slot], ag_sem.at[slot])
        remote(gath.at[slot], gath.at[slot], ag_send, ag_sem.at[slot], partner)
    for k in range(chips):
        slot = 2 * peer(k) + 1 - core
        wait(gath.at[slot], ag_sem.at[slot])

    def output_rows(index):
        weights = wout[pl.ds(pl.multiple_of(index * local_ch, local_ch), local_ch), :]
        return dot(gath[index], weights)

    total = output_rows(0)
    for i in range(1, chans):
        total += output_rows(i)
    o_out[...] = total.astype(BF16)
    out_copy = pltpu.make_async_copy(o_out, out_h, store_sem.at[0])
    out_copy.start()

    arrive(r_gtaps, 5)
    o_gtaps[...] = from_pieces(r_gtaps) * scale
    gtaps_copy = pltpu.make_async_copy(o_gtaps, gtaps_h, store_sem.at[1])
    gtaps_copy.start()

    gtok_copies = []
    for h in (0, 1):
        cut = columns(o_gtok, h)
        o_gtok[:, cut] = collect(b_own, b_in, b_i_sem, h).astype(BF16)
        copy = pltpu.make_async_copy(
            o_gtok.at[:, cut], gtok_h.at[:, cut], store_sem.at[2 + h]
        )
        copy.start()
        gtok_copies.append(copy)

    for n, buf in enumerate((s_taps, s_pre, s_grad, s_conv, s_gpre, s_gtaps)):
        wait(buf.at[pl.ds(0, ranks - 1)], seq_send.at[n])
    wait(a_send, pair_send.at[0])
    wait(b_send, pair_send.at[1])
    wait(a_sum, x_send.at[0])
    wait(b_sum, x_send.at[1])
    wait(gath.at[pl.ds(0, 7)], ag_send)
    out_copy.wait()
    gtaps_copy.wait()
    for copy in gtok_copies:
        copy.wait()


def place(a, b, c, d, e, f, va, vb, vc, load_sem, store_sem):
    loads, stores = [], []
    for i, (src, held, dst) in enumerate(((a, va, d), (b, vb, e), (c, vc, f))):
        count = src.shape[0] // 4
        for j in range(4):
            cut = pl.ds(j * count, count)
            loads.append(
                pltpu.make_async_copy(src.at[cut], held.at[cut], load_sem.at[i, j])
            )
            stores.append(
                pltpu.make_async_copy(held.at[cut], dst.at[cut], store_sem.at[i, j])
            )
    for load in loads:
        load.start()
    for load, store in zip(loads, stores):
        load.wait()
        store.start()
    for store in stores:
        store.wait()


def on_device(ranks, chans, tokens, in_weight, filter_taps, skip_gain, out_weight, grad_out):
    block, width = tokens.shape
    local_ch = in_weight.shape[2]
    feats = grad_out.shape[1]
    per = local_ch // ranks
    chips = chans // 2
    half = 2 * ranks * per
    weight = jnp.transpose(in_weight, (1, 0, 2))
    constants = tables(ranks, per)
    hbm = pl.BlockSpec(memory_space=pl.ANY)
    vmem = pl.BlockSpec(memory_space=pltpu.VMEM)
    piece = (ranks, 2 * per, LANES)
    chunk = (chips, block, local_ch)
    wide = (chips, block, feats)

    def travel(count):
        shapes = (
            (3, 2, block, count // 2),
            (2, 2, block // 2, count // 2),
            (2, 2, block, count // 2),
        )
        return [pltpu.VMEM(shape, BF16) for shape in shapes]

    scratch = [
        pltpu.VMEM(tokens.shape, BF16),
        pltpu.VMEM(weight.shape, BF16),
        pltpu.VMEM(filter_taps.shape, F32),
        pltpu.VMEM(out_weight.shape, BF16),
        pltpu.VMEM(grad_out.shape, BF16),
        pltpu.VMEM((2 * half, half), BF16),
        pltpu.VMEM((half, 2 * half), BF16),
        pltpu.VMEM((2 * LANES, 2 * LANES), BF16),
        pltpu.VMEM((2 * LANES, 2 * LANES), BF16),
        pltpu.VMEM((half, LANES), F32),
        pltpu.VMEM((half, LANES), F32),
        pltpu.VMEM((3, block, local_ch), BF16),
        pltpu.VMEM((block, local_ch), F32),
        pltpu.VMEM((block, local_ch), F32),
        pltpu.VMEM((block, local_ch), F32),
        pltpu.VMEM((half, 2 * LANES), F32),
        pltpu.VMEM((half, 2 * LANES), F32),
        pltpu.VMEM((half, 2 * LANES), F32),
        pltpu.VMEM((2, block, feats), F32),
        *[pltpu.VMEM(piece, BF16) for _ in range(12)],
        pltpu.VMEM(chunk, BF16),
        pltpu.VMEM(chunk, BF16),
        pltpu.VMEM(chunk, F32),
        *travel(local_ch),
        pltpu.VMEM((chans, block, local_ch), BF16),
        pltpu.VMEM((3, block, local_ch), BF16),
        pltpu.VMEM(wide, BF16),
        pltpu.VMEM(wide, BF16),
        pltpu.VMEM(wide, F32),
        *travel(feats),
        pltpu.VMEM((block, feats), BF16),
        pltpu.VMEM((block, feats), BF16),
        pltpu.VMEM((block, local_ch), F32),
        pltpu.SemaphoreType.DMA((13,)),
        pltpu.SemaphoreType.DMA((4,)),
        pltpu.SemaphoreType.DMA((6,)),
        pltpu.SemaphoreType.DMA((6,)),
        pltpu.SemaphoreType.DMA((2,)),
        pltpu.SemaphoreType.DMA((chips,)),
        pltpu.SemaphoreType.DMA((chips + 1,)),
        pltpu.SemaphoreType.DMA((2,)),
        pltpu.SemaphoreType.DMA((2, 2)),
        pltpu.SemaphoreType.DMA((2, 2)),
        pltpu.SemaphoreType.DMA((2, 2, 2)),
        pltpu.SemaphoreType.DMA((2, 2, 2)),
        pltpu.SemaphoreType.DMA,
        pltpu.SemaphoreType.DMA((chans,)),
    ]
    results = pl.pallas_call(
        functools.partial(kernel, ranks, chans),
        out_shape=(
            jax.ShapeDtypeStruct((block, feats), BF16),
            jax.ShapeDtypeStruct((block, feats), BF16),
            jax.ShapeDtypeStruct((block, local_ch), F32),
        ),
        in_specs=[hbm, hbm, hbm, vmem, hbm, hbm] + [hbm] * 6,
        out_specs=(hbm, hbm, hbm),
        scratch_shapes=scratch,
        compiler_params=pltpu.CompilerParams(
            collective_id=0, has_side_effects=True, vmem_limit_bytes=58 * 1024 * 1024
        ),
    )(
        tokens, weight, filter_taps, skip_gain.reshape(1, local_ch), out_weight, grad_out,
        *[jnp.asarray(table) for table in constants],
    )
    return pl.pallas_call(
        place,
        out_shape=tuple(jax.ShapeDtypeStruct(r.shape, r.dtype) for r in results),
        in_specs=[hbm] * 3,
        out_specs=(hbm,) * 3,
        scratch_shapes=[pltpu.VMEM(r.shape, r.dtype) for r in results]
        + [pltpu.SemaphoreType.DMA((3, 4))] * 2,
        compiler_params=pltpu.CompilerParams(vmem_limit_bytes=58 * 1024 * 1024),
    )(*results)


def solution(mesh):
    placed = (
        P("seq", None),
        P(None, None, "ch"),
        P("seq", "ch"),
        P("ch"),
        P(None, "ch"),
        P("seq", "ch"),
    )
    return jax.shard_map(
        functools.partial(on_device, mesh.shape["seq"], mesh.shape["ch"]),
        mesh=mesh,
        in_specs=placed,
        out_specs=(P("seq", "ch"), P("seq", "ch"), P("seq", "ch")),
        check_vma=False,
    )
```

```python
import functools
import math

import jax
import jax.numpy as jnp
import ml_dtypes
import numpy as np
from jax import lax
from jax.experimental import pallas as pl
from jax.experimental.pallas import tpu as pltpu
from jax.sharding import PartitionSpec as P

MESH = pl.DeviceIdType.MESH
F32 = jnp.float32
BF16 = jnp.bfloat16
LANES = 128


def tables(ranks, per):
    rows = 2 * ranks
    length = rows * LANES
    first = np.arange(rows)
    low = first + 0.25
    angle = 2.0 * np.pi * np.outer(low, first) / rows
    eye = np.eye(per)
    cross = np.concatenate(
        [np.kron(np.cos(angle), eye), np.kron(-np.sin(angle), eye)], axis=0
    )
    cross_back = cross.T / length
    turn = 2.0 * np.pi * np.outer(np.repeat(low, per), np.arange(LANES)) / length
    inner = 2.0 * np.pi * np.outer(np.arange(LANES), np.arange(LANES)) / LANES
    cosine, sine = np.cos(inner), np.sin(inner)
    local = np.block([[cosine, -sine], [sine, cosine]])
    narrow = ml_dtypes.bfloat16
    return (
        cross.astype(narrow),
        cross_back.astype(narrow),
        local.astype(narrow),
        local.T.astype(narrow),
        np.cos(turn).astype(np.float32),
        (-np.sin(turn)).astype(np.float32),
    )


def dot(left, right):
    return jnp.dot(left, right, preferred_element_type=F32)


def dot_nt(left, right):
    return lax.dot_general(
        left, right, (((1,), (1,)), ((), ())), preferred_element_type=F32
    )


def kernel(
    ranks,
    chans,
    *refs,
):
    (
        tok_h, win_h, taps_h, skip_ref, wout_h, gout_h,
        cross_h, back_h, local_h, unlocal_h, tr_h, ti_h,
        out_h, gtok_h, gtaps_h,
        tok, win, taps, wout, gout, cross, back, local, unlocal, tr, ti,
        mixed, pre, gg, gc, spec_t, spec_p, spec_g, early,
        s_taps, s_pre, s_grad, s_conv, s_gpre, s_gtaps,
        r_taps, r_pre, r_grad, r_conv, r_gpre, r_gtaps,
        a_send, a_got, a_own, a_sum, a_fwd, a_in,
        gath, gm,
        b_send, b_got, b_own, b_sum, b_fwd, b_in,
        o_out, o_gtok, o_gtaps,
        load_sem, store_sem, seq_send, seq_recv,
        pair_send, a_sem, b_sem, x_send, a_f_sem, b_f_sem, a_i_sem, b_i_sem,
        ag_send, ag_sem,
    ) = refs
    seq = lax.axis_index("seq")
    ch = lax.axis_index("ch")
    chips = chans // 2
    x, core = lax.div(ch, 2), lax.rem(ch, 2)
    partner = (seq, ch + 1 - 2 * core)
    block, width = tok.shape
    local_ch = win.shape[2]
    per = local_ch // ranks
    feats = gout.shape[1]
    half = ranks * 2 * per
    scale = (ranks * block) ** -0.5
    part = block // 2
    turns = 4 if ranks % 8 == 0 else 1
    some = ranks // 2

    def peer(step):
        return lax.rem(x + step, chips)

    def slot_of(rank):
        z, y = lax.div(rank, turns), lax.rem(rank, turns)
        return lax.rem(z, 2) * some + lax.div(z, 2) * turns + y

    def rank_of(slot):
        side, rest = lax.div(slot, some), lax.rem(slot, some)
        return (2 * lax.div(rest, turns) + side) * turns + lax.rem(rest, turns)

    mine = slot_of(seq)

    def rounds(send):
        first = ranks * 3 // 8
        lax.fori_loop(max(first, 1), ranks, send, 0, unroll=True)
        lax.fori_loop(1, first, send, 0, unroll=True)

    barrier = pltpu.get_barrier_semaphore()

    def greet(k, carry):
        pl.semaphore_signal(
            barrier, inc=1, device_id=(lax.rem(seq + k, ranks), ch), device_id_type=MESH
        )
        return carry

    rounds(greet)
    pl.semaphore_signal(barrier, inc=1, device_id=partner, device_id_type=MESH)
    for k in (1, 2, 3):
        pl.semaphore_signal(
            barrier, inc=1, device_id=(seq, 2 * peer(k) + core), device_id_type=MESH
        )

    loads = [
        (taps_h, taps), (gout_h, gout), (wout_h, wout), (tok_h, tok),
        (win_h.at[0], win.at[0]), (win_h.at[1], win.at[1]), (win_h.at[2], win.at[2]),
        (cross_h, cross), (local_h, local), (tr_h, tr), (ti_h, ti),
        (unlocal_h, unlocal), (back_h, back),
    ]
    copies = [
        pltpu.make_async_copy(src, dst, load_sem.at[i])
        for i, (src, dst) in enumerate(loads)
    ]
    for copy in copies[:3]:
        copy.start()

    def remote(src, dst, send, recv, device):
        copy = pltpu.make_async_remote_copy(
            src_ref=src, dst_ref=dst, send_sem=send, recv_sem=recv,
            device_id=device, device_id_type=MESH,
        )
        copy.start()

    def wait(ref, sem):
        pltpu.make_async_copy(ref, ref, sem).wait()

    def spread(buf, got, n):
        def send(k, carry):
            to = lax.rem(seq + k, ranks)
            remote(
                buf.at[slot_of(to)], got.at[seq], seq_send.at[n], seq_recv.at[n], (to, ch)
            )
            return carry

        rounds(send)
        got[seq] = buf[mine]

    def spread_side(buf, got, n, side):
        def send(k, carry):
            slot = side * some + lax.rem(mine + some * 3 // 8 + k, some)
            to = rank_of(slot)

            @pl.when(to != seq)
            def _():
                remote(
                    buf.at[slot], got.at[seq], seq_send.at[n], seq_recv.at[n], (to, ch)
                )

            return carry

        lax.fori_loop(0, some, send, 0, unroll=True)

    def give_back(buf, got, n):
        def send(k, carry):
            to = lax.rem(seq + k, ranks)
            remote(buf.at[to], got.at[mine], seq_send.at[n], seq_recv.at[n], (to, ch))
            return carry

        rounds(send)
        got[mine] = buf[seq]

    def arrive(got, n):
        wait(got.at[pl.ds(0, ranks - 1)], seq_recv.at[n])

    def to_pieces(value, buf, first):
        turned = value.T
        count = turned.shape[0] // per
        parts = [
            turned[:, i * LANES : (i + 1) * LANES].reshape(count, per, LANES)
            for i in range(2)
        ]
        buf[first : first + count] = jnp.concatenate(parts, axis=1).astype(BF16)

    def from_pieces(got):
        parts = got[...].astype(F32)
        turned = jnp.concatenate(
            [
                parts[:, i * per : (i + 1) * per, :].reshape(local_ch, LANES)
                for i in range(2)
            ],
            axis=1,
        )
        return turned.T

    def spectrum(got):
        flat = got[...].reshape(half, LANES)
        both = dot(cross[...], flat)
        re, im = both[:half], both[half:]
        cosine, sine = tr[...], ti[...]
        turned = jnp.concatenate(
            [re * cosine - im * sine, re * sine + im * cosine], axis=1
        )
        return dot(turned.astype(BF16), local[...])

    def inverse(re, im, buf):
        both = dot(jnp.concatenate([re, im], axis=1).astype(BF16), unlocal[...])
        re, im = both[:, :LANES], both[:, LANES:]
        cosine, sine = tr[...], ti[...]
        turned = jnp.concatenate(
            [re * cosine + im * sine, im * cosine - re * sine], axis=0
        )
        result = dot(back[...], turned.astype(BF16))
        buf[...] = result.astype(BF16).reshape(ranks, 2 * per, LANES)

    near = (1, 3)

    def rows(d):
        return pl.ds(d * part, part)

    def columns(ref, h):
        count = ref.shape[-1] // 2
        return slice(h * count, (h + 1) * count)

    def fold(own, got, sem, k):
        to = peer(k)
        wait(got.at[to], sem.at[to])
        own[to] = own[to] + got[to].astype(F32)

    def far(own, sums, fwd, f_sem, n, h):
        sums[0, h] = own[peer(2), :, columns(own, h)].astype(BF16)
        for d in (0, 1):
            remote(
                sums.at[0, h, rows(d)], fwd.at[d, h], x_send.at[n], f_sem.at[d, h],
                (seq, 2 * peer(near[d]) + core),
            )

    def plain(own, sums, into, i_sem, n, h):
        for d in (0, 1):
            to = peer(near[d])
            sums[1 + d, h, rows(1 - d)] = own[
                to, rows(1 - d), columns(own, h)
            ].astype(BF16)
            remote(
                sums.at[1 + d, h, rows(1 - d)], into.at[d, h, rows(1 - d)],
                x_send.at[n], i_sem.at[0, d, h], (seq, 2 * to + core),
            )

    def onward(own, sums, fwd, f_sem, into, i_sem, n, h):
        for d in (0, 1):
            to = peer(near[d])
            wait(fwd.at[d, h], f_sem.at[d, h])
            sums[1 + d, h, rows(d)] = (
                own[to, rows(d), columns(own, h)] + fwd[d, h].astype(F32)
            ).astype(BF16)
            remote(
                sums.at[1 + d, h, rows(d)], into.at[d, h, rows(d)],
                x_send.at[n], i_sem.at[1, d, h], (seq, 2 * to + core),
            )

    def collect(own, into, i_sem, h):
        for d in (0, 1):
            wait(into.at[d, h, rows(1 - d)], i_sem.at[0, d, h])
            wait(into.at[d, h, rows(d)], i_sem.at[1, d, h])
        return own[x, :, columns(own, h)] + (
            into[0, h].astype(F32) + into[1, h].astype(F32)
        )

    def feature_chunk(index):
        weights = wout[pl.ds(pl.multiple_of(index * local_ch, local_ch), local_ch), :]
        return dot_nt(gout[...], weights)

    copies[0].wait()
    for copy in copies[3:]:
        copy.start()
    copies[1].wait()
    copies[2].wait()

    def a_chunk(k):
        to = peer(k)
        a_send[to] = feature_chunk(2 * to + 1 - core).astype(BF16)

    def a_leave(k):
        to = peer(k)
        remote(a_send.at[to], a_got.at[to], pair_send.at[0], a_sem.at[to], partner)

    a_chunk(2)
    pl.semaphore_wait(barrier, ranks - 1 + 1 + 3)
    a_leave(2)
    for k in (1, 3, 0):
        a_chunk(k)
    for k in (1, 3, 0):
        a_leave(k)
    to_pieces(taps[...] * scale, s_taps, 0)
    spread(s_taps, r_taps, 0)
    for k in (2, 1, 3, 0):
        to = peer(k)
        a_own[to] = feature_chunk(2 * to + core)
    fold(a_own, a_got, a_sem, 2)
    far(a_own, a_sum, a_fwd, a_f_sem, 0, 0)
    far(a_own, a_sum, a_fwd, a_f_sem, 0, 1)

    copies[3].wait()
    copies[4].wait()
    mixed[0] = dot(tok[...], win[0]).astype(BF16)
    fold(a_own, a_got, a_sem, 1)
    fold(a_own, a_got, a_sem, 3)
    plain(a_own, a_sum, a_in, a_i_sem, 0, 0)
    plain(a_own, a_sum, a_in, a_i_sem, 0, 1)
    copies[5].wait()
    mixed[1] = dot(tok[...], win[1]).astype(BF16)
    pre[...] = mixed[1].astype(F32) * mixed[0].astype(F32)
    to_pieces(pre[...], s_pre, 0)
    spread(s_pre, r_pre, 1)
    onward(a_own, a_sum, a_fwd, a_f_sem, a_in, a_i_sem, 0, 0)
    onward(a_own, a_sum, a_fwd, a_f_sem, a_in, a_i_sem, 0, 1)
    fold(a_own, a_got, a_sem, 0)
    copies[6].wait()
    mixed[2] = dot(tok[...], win[2]).astype(BF16)

    for h in (0, 1):
        cut = columns(gg, h)
        gg[:, cut] = collect(a_own, a_in, a_i_sem, h)
        gc[:, cut] = gg[:, cut] * mixed[2, :, cut].astype(F32)
        to_pieces(gc[:, cut], s_grad, h * some)
        spread_side(s_grad, r_grad, 2, h)
    r_grad[seq] = s_grad[mine]

    for copy in copies[7:]:
        copy.wait()
    arrive(r_taps, 0)
    spec_t[...] = spectrum(r_taps)
    arrive(r_pre, 1)
    spec_p[...] = spectrum(r_pre)
    t_re, t_im = spec_t[:, :LANES], spec_t[:, LANES:]
    p_re, p_im = spec_p[:, :LANES], spec_p[:, LANES:]
    inverse(t_re * p_re - t_im * p_im, t_re * p_im + t_im * p_re, s_conv)
    give_back(s_conv, r_conv, 3)
    arrive(r_grad, 2)
    spec_g[...] = spectrum(r_grad)
    g_re, g_im = spec_g[:, :LANES], spec_g[:, LANES:]
    t_re, t_im = spec_t[:, :LANES], spec_t[:, LANES:]
    inverse(t_re * g_re + t_im * g_im, t_re * g_im - t_im * g_re, s_gpre)
    give_back(s_gpre, r_gpre, 4)
    p_re, p_im = spec_p[:, :LANES], spec_p[:, LANES:]
    g_re, g_im = spec_g[:, :LANES], spec_g[:, LANES:]
    inverse(p_re * g_re + p_im * g_im, p_re * g_im - p_im * g_re, s_gtaps)

    arrive(r_conv, 3)
    conv = from_pieces(r_conv) + skip_ref[...] * pre[...]
    gath[ch] = (mixed[2].astype(F32) * conv).astype(BF16)
    for k in (2, 1, 3):
        remote(
            gath.at[ch], gath.at[ch], ag_send, ag_sem.at[ch], (seq, 2 * peer(k) + core)
        )
    remote(gath.at[ch], gath.at[ch], ag_send, ag_sem.at[ch], partner)
    gm[2] = (gg[...] * conv).astype(BF16)
    for i in (0, 1):
        owner = 2 * peer(2) + (core if i else 1 - core)
        span = pl.ds(pl.multiple_of(owner * feats, feats), feats)
        early[i] = dot_nt(gm[2], win[2, span, :])

    arrive(r_gpre, 4)
    grad_pre = from_pieces(r_gpre) + skip_ref[...] * gc[...]
    gm[0] = (grad_pre * mixed[1].astype(F32)).astype(BF16)
    gm[1] = (grad_pre * mixed[0].astype(F32)).astype(BF16)

    def input_chunk(index):
        span = pl.ds(pl.multiple_of(index * feats, feats), feats)
        total = dot_nt(gm[0], win[0, span, :])
        total += dot_nt(gm[1], win[1, span, :])
        return total + dot_nt(gm[2], win[2, span, :])

    def to_partner(k):
        to = peer(k)
        b_send[to] = input_chunk(2 * to + 1 - core).astype(BF16)
        remote(b_send.at[to], b_got.at[to], pair_send.at[1], b_sem.at[to], partner)

    def to_self(k):
        b_own[peer(k)] = input_chunk(2 * peer(k) + core)

    def half_chunk(i, h):
        owner = 2 * peer(2) + (core if i else 1 - core)
        count = feats // 2
        span = pl.ds(pl.multiple_of(owner * feats + h * count, count), count)
        total = early[i, :, columns(early, h)] + dot_nt(gm[0], win[0, span, :])
        return total + dot_nt(gm[1], win[1, span, :])

    to = peer(2)
    pair_sem = (b_sem.at[to], b_sem.at[chips])

    def half_to_partner(h):
        cut = columns(b_send, h)
        b_send[to, :, cut] = half_chunk(0, h).astype(BF16)
        remote(
            b_send.at[to, :, cut], b_got.at[to, :, cut], pair_send.at[1], pair_sem[h],
            partner,
        )

    def half_far(h):
        cut = columns(b_own, h)
        wait(b_got.at[to, :, cut], pair_sem[h])
        b_own[to, :, cut] = b_own[to, :, cut] + b_got[to, :, cut].astype(F32)
        far(b_own, b_sum, b_fwd, b_f_sem, 1, h)

    half_to_partner(0)
    b_own[to, :, columns(b_own, 0)] = half_chunk(1, 0)
    half_to_partner(1)
    half_far(0)
    b_own[to, :, columns(b_own, 1)] = half_chunk(1, 1)
    half_far(1)
    to_partner(1)
    to_partner(3)
    give_back(s_gtaps, r_gtaps, 5)
    to_self(1)
    to_self(3)
    fold(b_own, b_got, b_sem, 1)
    fold(b_own, b_got, b_sem, 3)
    for h in (0, 1):
        plain(b_own, b_sum, b_in, b_i_sem, 1, h)
    to_partner(0)
    onward(b_own, b_sum, b_fwd, b_f_sem, b_in, b_i_sem, 1, 0)
    to_self(0)
    fold(b_own, b_got, b_sem, 0)
    onward(b_own, b_sum, b_fwd, b_f_sem, b_in, b_i_sem, 1, 1)

    for k in (1, 3, 2):
        slot = 2 * peer(k) + core
        wait(gath.at[slot], ag_sem.at[slot])
        remote(gath.at[slot], gath.at[slot], ag_send, ag_sem.at[slot], partner)
    for k in range(chips):
        slot = 2 * peer(k) + 1 - core
        wait(gath.at[slot], ag_sem.at[slot])

    def output_rows(index):
        weights = wout[pl.ds(pl.multiple_of(index * local_ch, local_ch), local_ch), :]
        return dot(gath[index], weights)

    total = output_rows(0)
    for i in range(1, chans):
        total += output_rows(i)
    o_out[...] = total.astype(BF16)
    out_copy = pltpu.make_async_copy(o_out, out_h, store_sem.at[0])
    out_copy.start()

    arrive(r_gtaps, 5)
    o_gtaps[...] = from_pieces(r_gtaps) * scale
    gtaps_copy = pltpu.make_async_copy(o_gtaps, gtaps_h, store_sem.at[1])
    gtaps_copy.start()

    gtok_copies = []
    for h in (0, 1):
        cut = columns(o_gtok, h)
        o_gtok[:, cut] = collect(b_own, b_in, b_i_sem, h).astype(BF16)
        copy = pltpu.make_async_copy(
            o_gtok.at[:, cut], gtok_h.at[:, cut], store_sem.at[2 + h]
        )
        copy.start()
        gtok_copies.append(copy)

    for n, buf in enumerate((s_taps, s_pre, s_grad, s_conv, s_gpre, s_gtaps)):
        wait(buf.at[pl.ds(0, ranks - 1)], seq_send.at[n])
    wait(a_send, pair_send.at[0])
    wait(b_send, pair_send.at[1])
    wait(a_sum, x_send.at[0])
    wait(b_sum, x_send.at[1])
    wait(gath.at[pl.ds(0, 7)], ag_send)
    out_copy.wait()
    gtaps_copy.wait()
    for copy in gtok_copies:
        copy.wait()


def place(a, b, c, d, e, f, va, vb, vc, load_sem, store_sem):
    loads, stores = [], []
    for i, (src, held, dst) in enumerate(((a, va, d), (b, vb, e), (c, vc, f))):
        count = src.shape[0] // 4
        for j in range(4):
            cut = pl.ds(j * count, count)
            loads.append(
                pltpu.make_async_copy(src.at[cut], held.at[cut], load_sem.at[i, j])
            )
            stores.append(
                pltpu.make_async_copy(held.at[cut], dst.at[cut], store_sem.at[i, j])
            )
    for load in loads:
        load.start()
    for load, store in zip(loads, stores):
        load.wait()
        store.start()
    for store in stores:
        store.wait()


def on_device(ranks, chans, tokens, in_weight, filter_taps, skip_gain, out_weight, grad_out):
    block, width = tokens.shape
    local_ch = in_weight.shape[2]
    feats = grad_out.shape[1]
    per = local_ch // ranks
    chips = chans // 2
    half = 2 * ranks * per
    weight = jnp.transpose(in_weight, (1, 0, 2))
    constants = tables(ranks, per)
    hbm = pl.BlockSpec(memory_space=pl.ANY)
    vmem = pl.BlockSpec(memory_space=pltpu.VMEM)
    piece = (ranks, 2 * per, LANES)
    chunk = (chips, block, local_ch)
    wide = (chips, block, feats)

    def travel(count):
        shapes = (
            (3, 2, block, count // 2),
            (2, 2, block // 2, count // 2),
            (2, 2, block, count // 2),
        )
        return [pltpu.VMEM(shape, BF16) for shape in shapes]

    scratch = [
        pltpu.VMEM(tokens.shape, BF16),
        pltpu.VMEM(weight.shape, BF16),
        pltpu.VMEM(filter_taps.shape, F32),
        pltpu.VMEM(out_weight.shape, BF16),
        pltpu.VMEM(grad_out.shape, BF16),
        pltpu.VMEM((2 * half, half), BF16),
        pltpu.VMEM((half, 2 * half), BF16),
        pltpu.VMEM((2 * LANES, 2 * LANES), BF16),
        pltpu.VMEM((2 * LANES, 2 * LANES), BF16),
        pltpu.VMEM((half, LANES), F32),
        pltpu.VMEM((half, LANES), F32),
        pltpu.VMEM((3, block, local_ch), BF16),
        pltpu.VMEM((block, local_ch), F32),
        pltpu.VMEM((block, local_ch), F32),
        pltpu.VMEM((block, local_ch), F32),
        pltpu.VMEM((half, 2 * LANES), F32),
        pltpu.VMEM((half, 2 * LANES), F32),
        pltpu.VMEM((half, 2 * LANES), F32),
        pltpu.VMEM((2, block, feats), F32),
        *[pltpu.VMEM(piece, BF16) for _ in range(12)],
        pltpu.VMEM(chunk, BF16),
        pltpu.VMEM(chunk, BF16),
        pltpu.VMEM(chunk, F32),
        *travel(local_ch),
        pltpu.VMEM((chans, block, local_ch), BF16),
        pltpu.VMEM((3, block, local_ch), BF16),
        pltpu.VMEM(wide, BF16),
        pltpu.VMEM(wide, BF16),
        pltpu.VMEM(wide, F32),
        *travel(feats),
        pltpu.VMEM((block, feats), BF16),
        pltpu.VMEM((block, feats), BF16),
        pltpu.VMEM((block, local_ch), F32),
        pltpu.SemaphoreType.DMA((13,)),
        pltpu.SemaphoreType.DMA((4,)),
        pltpu.SemaphoreType.DMA((6,)),
        pltpu.SemaphoreType.DMA((6,)),
        pltpu.SemaphoreType.DMA((2,)),
        pltpu.SemaphoreType.DMA((chips,)),
        pltpu.SemaphoreType.DMA((chips + 1,)),
        pltpu.SemaphoreType.DMA((2,)),
        pltpu.SemaphoreType.DMA((2, 2)),
        pltpu.SemaphoreType.DMA((2, 2)),
        pltpu.SemaphoreType.DMA((2, 2, 2)),
        pltpu.SemaphoreType.DMA((2, 2, 2)),
        pltpu.SemaphoreType.DMA,
        pltpu.SemaphoreType.DMA((chans,)),
    ]
    results = pl.pallas_call(
        functools.partial(kernel, ranks, chans),
        out_shape=(
            jax.ShapeDtypeStruct((block, feats), BF16),
            jax.ShapeDtypeStruct((block, feats), BF16),
            jax.ShapeDtypeStruct((block, local_ch), F32),
        ),
        in_specs=[hbm, hbm, hbm, vmem, hbm, hbm] + [hbm] * 6,
        out_specs=(hbm, hbm, hbm),
        scratch_shapes=scratch,
        compiler_params=pltpu.CompilerParams(
            collective_id=0, has_side_effects=True, vmem_limit_bytes=58 * 1024 * 1024
        ),
    )(
        tokens, weight, filter_taps, skip_gain.reshape(1, local_ch), out_weight, grad_out,
        *[jnp.asarray(table) for table in constants],
    )
    return pl.pallas_call(
        place,
        out_shape=tuple(jax.ShapeDtypeStruct(r.shape, r.dtype) for r in results),
        in_specs=[hbm] * 3,
        out_specs=(hbm,) * 3,
        scratch_shapes=[pltpu.VMEM(r.shape, r.dtype) for r in results]
        + [pltpu.SemaphoreType.DMA((3, 4))] * 2,
        compiler_params=pltpu.CompilerParams(vmem_limit_bytes=58 * 1024 * 1024),
    )(*results)


def solution(mesh):
    placed = (
        P("seq", None),
        P(None, None, "ch"),
        P("seq", "ch"),
        P("ch"),
        P(None, "ch"),
        P("seq", "ch"),
    )
    return jax.shard_map(
        functools.partial(on_device, mesh.shape["seq"], mesh.shape["ch"]),
        mesh=mesh,
        in_specs=placed,
        out_specs=(P("seq", "ch"), P("seq", "ch"), P("seq", "ch")),
        check_vma=False,
    )
```
